256 devices in a mesh: ctx: 16 (over y_lo, z), fsdp: 16 (over y_hi, x, core).
Axes of the slice: x: 4, y: 4 (y_hi: 2, y_lo: 2; y = y_hi * 2 + y_lo), z: 8, core: 2. Of those that a mesh axis runs over, the one named last changes fastest.
Arguments:
- hidden_in: bfloat16 [16, 2048, 8192], P('fsdp', 'ctx'), may hold values from -600 to 600
- queries: bfloat16 [16, 2048, 4096], P('fsdp', 'ctx'), may hold values from -100 to 100
- kv_weight: bfloat16 [8192, 1024], P('fsdp'), may hold values from -0.0625 to 0.0625
- kv_bias: float32 [1024], replicated, may hold values from -3 to 3
- norm_gain: float32 [8192], replicated, may hold values from 0.1 to 1.9
- block_mask: int32 [16, 16, 16], P('fsdp'), may hold values from 0 to 1, as said below
Outputs:
- attended: bfloat16 [16, 2048, 4096], P('fsdp', 'ctx')
The draws below stay inside these ranges and needn't reach their ends.
Inputs may be any that keep to these rules, and one draw needn't show every extreme that they name: block_mask is 1 on the diagonal and 0 above it; the first block of a pack is visible to every block.
All inputs are finite; a program needn't handle non-finite values.
Results may differ from the reference program's by a relative error of at most 0.0056.
Values may be sent and summed in bfloat16 or wider, within the bound.
No kernel may reach another device: no remote copies, remote signals or barrier semaphores. Data moves between devices by JAX's collectives and lax.ppermute only.
A program may use at most 64 MiB of HBM per device.

```python
import math
import jax
import jax.numpy as jnp
from jax import lax

D = 8192
H = 32
KVH = 4
HD = 128
BLK = 128
LENGTH = 2048
SEQS = 16
NB = 16
KV2 = 1024


def draw_hidden_in(key, part):
    key = jax.random.fold_in(key, 3)
    shape_all = (SEQS, LENGTH, D)
    column_scale = jnp.exp(jax.random.uniform(jax.random.fold_in(key, 1), (D,), jnp.float32, 0.0, math.log(10.0)))
    row_scale = jnp.exp(jax.random.uniform(jax.random.fold_in(key, 2), (SEQS, LENGTH, 1), jnp.float32, 0.0, math.log(10.0)))
    base_values = jnp.clip(jax.random.normal(jax.random.fold_in(key, 4), shape_all, jnp.float32), -6.0, 6.0)
    return (base_values * column_scale * row_scale).astype(jnp.bfloat16)


def draw_queries(key, part):
    key = jax.random.fold_in(key, 11)
    shape_all = (SEQS, LENGTH, H * HD)
    base_values = jnp.clip(jax.random.normal(jax.random.fold_in(key, 1), shape_all, jnp.float32), -6.0, 6.0)
    return base_values.astype(jnp.bfloat16)


def draw_block_mask(key, part):
    key = jax.random.fold_in(key, 5)

    def one_pack(pack_index):
        pack_key = jax.random.fold_in(key, pack_index)
        block_ids = jnp.arange(NB, dtype=jnp.int32)
        flips = jax.random.randint(jax.random.fold_in(pack_key, 1), (NB,), 0, 3)
        prompt_blocks = max(NB // 8, 1)
        starts = jnp.where(block_ids == 0, 1, jnp.where(block_ids < prompt_blocks, 0, (flips == 0).astype(jnp.int32)))
        segment = jnp.cumsum(starts).astype(jnp.int32) - 1
        picks = jax.random.randint(jax.random.fold_in(pack_key, 2), (NB,), 0, 1 << 20)
        parent = jnp.where(block_ids > 0, picks % jnp.maximum(block_ids, 1), 0).astype(jnp.int32)
        reach_start = (block_ids[:, None] == block_ids[None, :]).astype(jnp.int32)

        def climb(turn_index, state_in):
            current, reach = state_in
            current = parent[current]
            reach = jnp.maximum(reach, (current[:, None] == block_ids[None, :]).astype(jnp.int32))
            return (current, reach)
        unused, reach = lax.fori_loop(0, NB, climb, (block_ids, reach_start))
        seen = reach[segment[:, None], segment[None, :]]
        lower_part = block_ids[None, :] <= block_ids[:, None]
        return jnp.where(lower_part, seen, 0).astype(jnp.int32)
    return lax.map(one_pack, jnp.arange(SEQS, dtype=jnp.int32))


def shard_levels(stream_key, shape, split, low, top_value):
    factor_of, own = 1.0, jax.random.fold_in(stream_key, 6)
    for dim, parts in split:
        draws = jnp.exp(jax.random.uniform(jax.random.fold_in(own, dim), (parts,), jnp.float32, low / len(split), top_value / len(split)))
        factor_of = factor_of * jnp.repeat(draws, shape[dim] // parts).reshape([-1 if axis == dim else 1 for axis in range(len(shape))])
    return factor_of


def scatter_about(own_key, extent, width, most, shards=(), held_as=jnp.bfloat16):
    level = shard_levels(own_key, extent, shards, -0.22, 0.18) if shards else 1.0
    values = jax.random.normal(own_key, extent, jnp.float32) * width * level
    return jnp.minimum(jnp.maximum(values, -most), most).astype(held_as)


def setup_inputs(seed: int = 0) -> dict:
    arg_keys = jax.random.split(jax.random.key(seed), 7)
    return {
        "hidden_in": draw_hidden_in(jax.random.fold_in(arg_keys[6], 71), 0),
        "queries": draw_queries(jax.random.fold_in(arg_keys[6], 71), 0),
        "kv_weight": scatter_about(arg_keys[2], (D, KV2), D ** -0.5, 0.0625, ((0, 16),)),
        "kv_bias": scatter_about(arg_keys[3], (KV2,), 0.5, 3.0, (), jnp.float32),
        "norm_gain": jnp.clip(1.0 + 0.18 * jax.random.normal(arg_keys[4], (D,), jnp.float32), 0.1, 1.9),
        "block_mask": draw_block_mask(jax.random.fold_in(arg_keys[6], 71), 0),
    }


def rotary(raw_keys, positions):
    key_count = raw_keys.shape[0]
    shaped = raw_keys.reshape(key_count, KVH, HD)
    half_dim = HD // 2
    inv_freq = jnp.exp(jnp.arange(half_dim, dtype=jnp.float32) * (-2.0 * math.log(1000000.0) / HD))
    angle = positions.astype(jnp.float32)[:, None] * inv_freq[None, :]
    cosine = jnp.cos(angle)[:, None, :]
    sine_part = jnp.sin(angle)[:, None, :]
    first_half = shaped[..., :half_dim]
    second_half = shaped[..., half_dim:]
    turned = jnp.concatenate([first_half * cosine - second_half * sine_part, second_half * cosine + first_half * sine_part], axis=-1)
    return turned.reshape(key_count, KVH * HD)

def reference(hidden_in, queries, kv_weight, kv_bias, norm_gain, block_mask):
    per_group = H // KVH

    def one_pack(inputs):
        hidden_rows, query_rows, mask_rows = inputs
        wide_rows = hidden_rows.astype(jnp.float32)
        inv_rms = lax.rsqrt(lax.optimization_barrier(jnp.mean(wide_rows * wide_rows, axis=-1, keepdims=True)) + 1e-06)
        normed = (wide_rows * inv_rms * norm_gain.astype(jnp.float32)).astype(jnp.bfloat16)
        projected = jnp.dot(normed, kv_weight, preferred_element_type=jnp.float32) + kv_bias.astype(jnp.float32)
        positions = jnp.arange(LENGTH, dtype=jnp.int32)
        key_rows = rotary(projected[:, :KVH * HD], positions).astype(jnp.bfloat16)
        value_rows = projected[:, KVH * HD:].astype(jnp.bfloat16)
        block_of = positions // BLK
        visible = (mask_rows[block_of][:, block_of] == 1) & (positions[None, :] <= positions[:, None])
        query_heads = query_rows.reshape(LENGTH, KVH, per_group, HD)
        key_heads = key_rows.reshape(LENGTH, KVH, HD)
        value_heads = value_rows.reshape(LENGTH, KVH, HD)

        def one_head(head_index):
            head_query = jnp.take(query_heads, head_index, axis=1).astype(jnp.float32)
            head_key = jnp.take(key_heads, head_index, axis=1).astype(jnp.float32)
            head_value = jnp.take(value_heads, head_index, axis=1).astype(jnp.float32)
            scores = jnp.einsum('tgd,ud->gtu', head_query, head_key) / math.sqrt(HD)
            row_top = lax.optimization_barrier(jnp.max(jnp.where(visible[None], scores, -jnp.inf), axis=-1, keepdims=True))
            weights = jnp.where(visible[None], jnp.exp(scores - row_top), 0.0)
            totals = lax.optimization_barrier(jnp.sum(weights, axis=-1, keepdims=True))
            rounded_weights = lax.optimization_barrier(weights.astype(jnp.bfloat16)).astype(jnp.float32)
            mixed_out = jnp.einsum('gtu,ud->gtd', rounded_weights, head_value)
            return (mixed_out / totals).astype(jnp.bfloat16)
        all_heads = lax.map(one_head, jnp.arange(KVH, dtype=jnp.int32))
        return all_heads.transpose(2, 0, 1, 3).reshape(LENGTH, H * HD)
    return lax.map(one_pack, (hidden_in, queries, block_mask))
```

```python
import math

import jax
import jax.numpy as jnp
from jax import lax
from jax.experimental import pallas as pl
from jax.experimental.pallas import tpu as pltpu
from jax.sharding import PartitionSpec as P

H = 32
KVH = 4
HD = 128
BLK = 128
D = 8192
GW = (H // KVH) * HD
LOW = -1e30
SCALE = math.log2(math.e) / math.sqrt(HD)
BF = jnp.bfloat16
F32 = jnp.float32


def x_pairs(k):
    return [(f, (f & 8) | ((((f >> 1) + k) & 3) << 1) | (f & 1)) for f in range(16)]


CORE_PAIRS = [(f, f ^ 1) for f in range(16)]
DIAG_PAIRS = [(i, i ^ (8 * 16) ^ 8) for i in range(256)]


def member_pairs(k):
    flip = ((k >> 1) << 3) | (k & 1)
    return [(c, c ^ flip) for c in range(16)]


def z_pairs(k):
    return [(c, (c & 8) | ((c + k) & 7)) for c in range(16)]


def norm_kernel(pos_ref, x_ref, gain_ref, *outs):
    xi, yhi, core = pos_ref[0], pos_ref[1], pos_ref[2]
    total = None
    for j in range(8):
        part = x_ref[:, j * 1024 : (j + 1) * 1024].astype(F32)
        part = part * part
        for i in range(8):
            piece = part[:, i * 128 : (i + 1) * 128]
            total = piece if total is None else total + piece
    inv = lax.rsqrt(jnp.sum(total, axis=-1, keepdims=True) / D + 1e-06)
    for k in range(4):
        for a in range(2):
            for b in range(2):
                src = (yhi ^ a) * 4096 + ((xi + k) & 3) * 1024 + (core ^ b) * 512
                cols = pl.ds(pl.multiple_of(src, 512), 512)
                wide = x_ref[:, cols].astype(F32)
                dst = (a * 2 + b) * 512
                outs[k][:, dst : dst + 512] = (wide * inv * gain_ref[:, cols]).astype(BF)


def norm_call(pos, hidden, gain):
    rows = hidden.shape[0]
    step = 32
    return pl.pallas_call(
        norm_kernel,
        grid_spec=pltpu.PrefetchScalarGridSpec(
            num_scalar_prefetch=1,
            grid=(rows // step,),
            in_specs=[
                pl.BlockSpec((step, D), lambda i, p: (i, 0)),
                pl.BlockSpec((1, D), lambda i, p: (0, 0)),
            ],
            out_specs=[pl.BlockSpec((step, D // 4), lambda i, p: (i, 0))] * 4,
        ),
        out_shape=[jax.ShapeDtypeStruct((rows, D // 4), BF)] * 4,
        compiler_params=pltpu.CompilerParams(vmem_limit_bytes=16 * 1024 * 1024),
        cost_estimate=pl.CostEstimate(flops=4 << 20, bytes_accessed=4 << 20, transcendentals=0),
        name="norm",
    )(pos, hidden, gain)


def kv_kernel(j_ref, own_ref, r1_ref, r2_ref, r3_ref, bias_ref, cos_ref, sin_ref, *outs):
    j = j_ref[0]

    def part(col):
        cols = pl.ds(pl.multiple_of(col, 128), 128)
        back = r1_ref[:, cols].astype(F32) + r2_ref[:, cols].astype(F32) + r3_ref[:, cols].astype(F32)
        return own_ref[:, cols] + back + bias_ref[:, cols]

    for k in range(4):
        head = j ^ k
        key = part(head * HD)
        turned = key * cos_ref[...] + pltpu.roll(key, HD // 2, 1) * sin_ref[...]
        outs[k][:, :HD] = turned.astype(BF)
        outs[k][:, HD:] = part(KVH * HD + head * HD).astype(BF)


def kv_call(j, own, r1, r2, r3, bias, cos, sin):
    vm = pl.BlockSpec(memory_space=pltpu.VMEM)
    return pl.pallas_call(
        kv_kernel,
        in_specs=[pl.BlockSpec(memory_space=pltpu.SMEM)] + [vm] * 7,
        out_specs=[vm] * 4,
        out_shape=[jax.ShapeDtypeStruct((own.shape[0], 2 * HD), BF)] * 4,
        compiler_params=pltpu.CompilerParams(vmem_limit_bytes=8 * 1024 * 1024),
        cost_estimate=pl.CostEstimate(flops=1 << 20, bytes_accessed=2 << 20, transcendentals=0),
        name="keys_values",
    )(j, own, r1, r2, r3, bias, cos, sin)


def attn_kernel(flag_ref, q_ref, *refs):
    kv_refs, out_ref, kv_all, top, acc = refs[:-4], refs[-4], refs[-3], refs[-2], refs[-1]
    qi = pl.program_id(0)
    chunks = kv_all.shape[0]
    heads = H // KVH

    @pl.when(qi == 0)
    def _():
        at = 0
        for ref in kv_refs:
            for i in range(ref.shape[0] // 256):
                kv_all[at] = ref[i * 256 : (i + 1) * 256, :]
                at += 1

    top[...] = jnp.full_like(top, LOW)
    acc[...] = jnp.zeros_like(acc)
    ones = jnp.ones((256, HD), BF)

    def update(c, valid):
        keys = kv_all[c, :, :HD]
        values = jnp.concatenate([kv_all[c, :, HD:], ones], axis=1)
        for h in range(heads):
            q = q_ref[0, :, h * HD : (h + 1) * HD]
            s = lax.dot_general(q, keys, (((1,), (1,)), ((), ())), preferred_element_type=F32)
            if valid is not None:
                s = jnp.where(valid, s, LOW)
            old = top[h]
            new = jnp.maximum(old, jnp.max(s, axis=-1, keepdims=True))
            top[h] = new
            shift = new * SCALE
            factor = jnp.exp2(old * SCALE - shift)
            p = jnp.exp2(s * SCALE - jnp.concatenate([shift, shift], axis=1))
            if valid is not None:
                p = jnp.where(valid, p, 0.0)
            add = jnp.dot(p.astype(BF), values, preferred_element_type=F32)
            acc[h] = acc[h] * jnp.concatenate([factor, factor], axis=1) + add

    def step(c, carry):
        f0 = flag_ref[qi, c * 2]
        f1 = flag_ref[qi, c * 2 + 1]
        plain = (f0 == 1) & (f1 == 1)

        @pl.when(plain)
        def _():
            update(c, None)

        @pl.when(jnp.logical_not(plain) & ((f0 + f1) > 0))
        def _():
            row = lax.broadcasted_iota(jnp.int32, (BLK, BLK), 0)
            col = lax.broadcasted_iota(jnp.int32, (BLK, BLK), 1)
            reach0 = jnp.where(f0 == 2, row, jnp.where(f0 == 1, BLK, -1))
            reach1 = jnp.where(f1 == 2, row, jnp.where(f1 == 1, BLK, -1))
            reach = jnp.concatenate([reach0, reach1], axis=1)
            update(c, jnp.concatenate([col, col], axis=1) <= reach)

        return carry

    lax.fori_loop(0, chunks, step, 0)
    for h in range(heads):
        out_ref[0, :, h * HD : (h + 1) * HD] = (acc[h, :, :HD] / acc[h, :, HD:]).astype(BF)


def attn_call(flags, q4, parts):
    chunks = sum(p.shape[0] for p in parts) // 256
    return pl.pallas_call(
        attn_kernel,
        grid_spec=pltpu.PrefetchScalarGridSpec(
            num_scalar_prefetch=1,
            grid=(4,),
            in_specs=[pl.BlockSpec((1, BLK, GW), lambda i, f: (i, 0, 0))]
            + [pl.BlockSpec(p.shape, lambda i, f: (0, 0)) for p in parts],
            out_specs=pl.BlockSpec((1, BLK, GW), lambda i, f: (i, 0, 0)),
            scratch_shapes=[
                pltpu.VMEM((chunks, 256, 2 * HD), BF),
                pltpu.VMEM((H // KVH, BLK, HD), F32),
                pltpu.VMEM((H // KVH, BLK, 2 * HD), F32),
            ],
        ),
        out_shape=jax.ShapeDtypeStruct((4, BLK, GW), BF),
        compiler_params=pltpu.CompilerParams(vmem_limit_bytes=24 * 1024 * 1024),
        cost_estimate=pl.CostEstimate(flops=6 << 30, bytes_accessed=4 << 20, transcendentals=8 << 20),
        name="attend",
    )(flags, q4, *parts)


def place_kernel(j_ref, *refs):
    out_ref = refs[-1]
    for k in range(4):
        cols = pl.ds(pl.multiple_of((j_ref[0] ^ k) * GW, GW), GW)
        out_ref[:, cols] = refs[k][...]


def place_call(j, parts):
    vm = pl.BlockSpec(memory_space=pltpu.VMEM)
    return pl.pallas_call(
        place_kernel,
        in_specs=[pl.BlockSpec(memory_space=pltpu.SMEM)] + [vm] * 4,
        out_specs=vm,
        out_shape=jax.ShapeDtypeStruct((BLK, H * HD), BF),
        compiler_params=pltpu.CompilerParams(vmem_limit_bytes=8 * 1024 * 1024),
        name="place",
    )(j, *parts)


def rotary_tables(start, count):
    half_dim = HD // 2
    positions = start + jnp.arange(count, dtype=jnp.int32)
    inv_freq = jnp.exp(jnp.arange(half_dim, dtype=F32) * (-2.0 * math.log(1000000.0) / HD))
    angle = positions.astype(F32)[:, None] * inv_freq[None, :]
    cosine, sine = jnp.cos(angle), jnp.sin(angle)
    return jnp.concatenate([cosine, cosine], 1), jnp.concatenate([-sine, sine], 1)


def on_device(hidden_in, queries, kv_weight, kv_bias, norm_gain, block_mask):
    f = lax.axis_index("fsdp")
    c = lax.axis_index("ctx")
    core, xi, yhi = f & 1, (f >> 1) & 3, f >> 3
    z, ylo = c & 7, c >> 3
    j = ylo * 2 + (z & 1)
    zq = z >> 1
    hidden = hidden_in.reshape(BLK, D)
    q = queries.reshape(BLK, H * HD)
    j1 = jnp.reshape(j, (1,))

    w_core = lax.ppermute(kv_weight, "fsdp", CORE_PAIRS)
    w_y = lax.ppermute(kv_weight, ("ctx", "fsdp"), DIAG_PAIRS)

    normed = norm_call(jnp.stack([xi, yhi, core]), hidden, norm_gain.reshape(1, D))
    n1 = lax.ppermute(normed[1], "fsdp", x_pairs(1))
    n3 = lax.ppermute(normed[3], "fsdp", x_pairs(3))
    n2 = lax.ppermute(normed[2], "fsdp", x_pairs(2))
    w_yc = lax.ppermute(w_y, "fsdp", CORE_PAIRS)

    q_parts = []
    for k in range(4):
        piece = lax.dynamic_slice(q, (0, (j ^ k) * GW), (BLK, GW))
        q_parts.append(piece if k == 0 else lax.ppermute(piece, "ctx", member_pairs(k)))
    q4 = jnp.stack(q_parts)

    weight = jnp.concatenate([kv_weight, w_core, w_y, w_yc], axis=0)
    own = jnp.dot(normed[0], weight, preferred_element_type=F32)
    back = []
    for got, k in ((n1, 3), (n3, 1), (n2, 2)):
        product = jnp.dot(got, weight, preferred_element_type=F32).astype(BF)
        back.append(lax.ppermute(product, "fsdp", x_pairs(k)))

    cos, sin = rotary_tables(c * BLK, BLK)
    kvs = kv_call(j1, own, back[0], back[1], back[2], kv_bias.reshape(1, -1), cos, sin)
    group = jnp.concatenate([kvs[0]] + [lax.ppermute(kvs[k], "ctx", member_pairs(k)) for k in (1, 2, 3)], axis=0)

    up = lax.ppermute(group, "ctx", z_pairs(2))
    down = lax.ppermute(group, "ctx", z_pairs(-2))
    far0 = lax.ppermute(up[:256], "ctx", z_pairs(2))
    far1 = lax.ppermute(down[256:], "ctx", z_pairs(-2))

    members = j ^ jnp.arange(4, dtype=jnp.int32)
    block_of = lambda at: (members >> 1) * 8 + 2 * at + (members & 1)
    q_ids = block_of(zq)
    u_ids = jnp.concatenate([q_ids, block_of((zq + 3) & 3), block_of((zq + 1) & 3), block_of((zq + 2) & 3)])
    table = block_mask.reshape(16, 16)
    seen = jnp.take(jnp.take(table, q_ids, axis=0), u_ids, axis=1) == 1
    order = q_ids[:, None] - u_ids[None, :]
    flags = jnp.where(order == 0, 2, jnp.where(order > 0, 1, 0)) * seen.astype(jnp.int32)

    out4 = attn_call(flags.astype(jnp.int32), q4, [group, up, down, far0, far1])
    parts = [out4[0]] + [lax.ppermute(out4[k], "ctx", member_pairs(k)) for k in (1, 2, 3)]
    return place_call(j1, parts).reshape(1, BLK, H * HD)


def solution(mesh):
    return jax.shard_map(
        on_device,
        mesh=mesh,
        in_specs=(
            P("fsdp", "ctx", None),
            P("fsdp", "ctx", None),
            P("fsdp", None),
            P(),
            P(),
            P("fsdp", None, None),
        ),
        out_specs=P("fsdp", "ctx", None),
        check_vma=False,
    )
```

```python
import math

import jax
import jax.numpy as jnp
from jax import lax
from jax.experimental import pallas as pl
from jax.experimental.pallas import tpu as pltpu
from jax.sharding import PartitionSpec as P

H = 32
KVH = 4
HD = 128
BLK = 128
D = 8192
GW = (H // KVH) * HD
LOW = -1e30
SCALE = math.log2(math.e) / math.sqrt(HD)
BF = jnp.bfloat16
F32 = jnp.float32


def x_pairs(k):
    return [(f, (f & 8) | ((((f >> 1) + k) & 3) << 1) | (f & 1)) for f in range(16)]


CORE_PAIRS = [(f, f ^ 1) for f in range(16)]
DIAG_PAIRS = [(i, i ^ (8 * 16) ^ 8) for i in range(256)]


def member_pairs(k):
    flip = ((k >> 1) << 3) | (k & 1)
    return [(c, c ^ flip) for c in range(16)]


def z_pairs(k):
    return [(c, (c & 8) | ((c + k) & 7)) for c in range(16)]


def norm_kernel(pos_ref, x_ref, gain_ref, *outs):
    xi, yhi, core = pos_ref[0], pos_ref[1], pos_ref[2]
    total = None
    for j in range(D // 128):
        part = x_ref[:, j * 128 : (j + 1) * 128].astype(F32)
        part = part * part
        total = part if total is None else total + part
    inv = lax.rsqrt(jnp.sum(total, axis=-1, keepdims=True) / D + 1e-06)
    for k in range(4):
        for a in range(2):
            for b in range(2):
                src = (yhi ^ a) * 4096 + ((xi + k) & 3) * 1024 + (core ^ b) * 512
                cols = pl.ds(pl.multiple_of(src, 512), 512)
                wide = x_ref[:, cols].astype(F32)
                dst = (a * 2 + b) * 512
                outs[k][:, dst : dst + 512] = (wide * inv * gain_ref[:, cols]).astype(BF)


def norm_call(pos, hidden, gain):
    rows = hidden.shape[0]
    step = 32
    return pl.pallas_call(
        norm_kernel,
        grid_spec=pltpu.PrefetchScalarGridSpec(
            num_scalar_prefetch=1,
            grid=(rows // step,),
            in_specs=[
                pl.BlockSpec((step, D), lambda i, p: (i, 0)),
                pl.BlockSpec((1, D), lambda i, p: (0, 0)),
            ],
            out_specs=[pl.BlockSpec((step, D // 4), lambda i, p: (i, 0))] * 4,
        ),
        out_shape=[jax.ShapeDtypeStruct((rows, D // 4), BF)] * 4,
        compiler_params=pltpu.CompilerParams(vmem_limit_bytes=60 * 1024 * 1024),
        cost_estimate=pl.CostEstimate(flops=4 << 20, bytes_accessed=4 << 20, transcendentals=0),
        name="norm",
    )(pos, hidden, gain)


def product_kernel(count, *refs):
    rows, weights, outs = refs[:count], refs[count : -count], refs[-count:]
    tokens = rows[0].shape[0]
    for n in range(4):
        cols = slice(n * 256, (n + 1) * 256)
        total = None
        at = 0
        for w_ref in weights:
            depth = w_ref.shape[0]
            left = jnp.concatenate([r[:, at : at + depth] for r in rows], axis=0)
            part = jnp.dot(left, w_ref[:, cols], preferred_element_type=F32)
            total = part if total is None else total + part
            at += depth
        for i in range(count):
            outs[i][:, cols] = total[i * tokens : (i + 1) * tokens].astype(outs[i].dtype)


def product_call(rows, weights, dtype, name):
    vm = pl.BlockSpec(memory_space=pltpu.VMEM)
    count, tokens = len(rows), rows[0].shape[0]
    return pl.pallas_call(
        lambda *refs: product_kernel(count, *refs),
        in_specs=[vm] * (count + len(weights)),
        out_specs=[vm] * count,
        out_shape=[jax.ShapeDtypeStruct((tokens, 1024), dtype)] * count,
        compiler_params=pltpu.CompilerParams(vmem_limit_bytes=24 * 1024 * 1024),
        cost_estimate=pl.CostEstimate(
            flops=count * tokens * 2048 * 2048, bytes_accessed=4 << 20, transcendentals=0
        ),
        name=name,
    )(*rows, *weights)


def kv_kernel(j_ref, own_ref, r1_ref, r2_ref, r3_ref, bias_ref, cos_ref, sin_ref, *outs):
    j = j_ref[0]

    def part(col):
        cols = pl.ds(pl.multiple_of(col, 128), 128)
        back = r1_ref[:, cols].astype(F32) + r2_ref[:, cols].astype(F32) + r3_ref[:, cols].astype(F32)
        return own_ref[:, cols] + back + bias_ref[:, cols]

    for k in range(4):
        head = j ^ k
        key = part(head * HD)
        turned = key * cos_ref[...] + pltpu.roll(key, HD // 2, 1) * sin_ref[...]
        outs[k][:, :HD] = turned.astype(BF)
        outs[k][:, HD:] = part(KVH * HD + head * HD).astype(BF)


def kv_call(j, own, r1, r2, r3, bias, cos, sin):
    vm = pl.BlockSpec(memory_space=pltpu.VMEM)
    return pl.pallas_call(
        kv_kernel,
        in_specs=[pl.BlockSpec(memory_space=pltpu.SMEM)] + [vm] * 7,
        out_specs=[vm] * 4,
        out_shape=[jax.ShapeDtypeStruct((own.shape[0], 2 * HD), BF)] * 4,
        compiler_params=pltpu.CompilerParams(vmem_limit_bytes=8 * 1024 * 1024),
        cost_estimate=pl.CostEstimate(flops=1 << 20, bytes_accessed=2 << 20, transcendentals=0),
        name="keys_values",
    )(j, own, r1, r2, r3, bias, cos, sin)


def attend_chunks(flag_ref, base, qi, q_ref, kv_refs, top, acc):
    heads = H // KVH
    ones = jnp.ones((256, HD), BF)

    def update(ref, low, valid):
        keys = ref[low : low + 256, :HD]
        values = jnp.concatenate([ref[low : low + 256, HD:], ones], axis=1)
        for h in range(heads):
            q = q_ref[qi, :, h * HD : (h + 1) * HD]
            s = lax.dot_general(q, keys, (((1,), (1,)), ((), ())), preferred_element_type=F32)
            if valid is not None:
                s = jnp.where(valid, s, LOW)
            old = top[h]
            new = jnp.maximum(old, jnp.max(s, axis=-1, keepdims=True))
            top[h] = new
            factor = jnp.exp2((old - new) * SCALE)
            p = jnp.exp2((s - jnp.concatenate([new, new], axis=1)) * SCALE)
            if valid is not None:
                p = jnp.where(valid, p, 0.0)
            add = jnp.dot(p.astype(BF), values, preferred_element_type=F32)
            acc[h] = acc[h] * jnp.concatenate([factor, factor], axis=1) + add

    c = base
    for ref in kv_refs:
        for low in range(0, ref.shape[0], 256):
            f0 = flag_ref[qi, c * 2]
            f1 = flag_ref[qi, c * 2 + 1]
            c += 1
            plain = (f0 == 1) & (f1 == 1)

            @pl.when(plain)
            def _(ref=ref, low=low):
                update(ref, low, None)

            @pl.when(jnp.logical_not(plain) & ((f0 + f1) > 0))
            def _(ref=ref, low=low, f0=f0, f1=f1):
                row = lax.broadcasted_iota(jnp.int32, (BLK, BLK), 0)
                col = lax.broadcasted_iota(jnp.int32, (BLK, BLK), 1)
                reach0 = jnp.where(f0 == 2, row, jnp.where(f0 == 1, BLK, -1))
                reach1 = jnp.where(f1 == 2, row, jnp.where(f1 == 1, BLK, -1))
                reach = jnp.concatenate([reach0, reach1], axis=1)
                update(ref, low, jnp.concatenate([col, col], axis=1) <= reach)


def attend_first_kernel(flag_ref, q_ref, kv_ref, top, acc):
    def step(qi, carry):
        top[qi] = jnp.full(top.shape[1:], LOW, F32)
        acc[qi] = jnp.zeros(acc.shape[1:], F32)
        attend_chunks(flag_ref, 0, qi, q_ref, [kv_ref], top.at[qi], acc.at[qi])
        return carry

    lax.fori_loop(0, 4, step, 0)


def attend_more_kernel(flag_ref, q_ref, up_ref, down_ref, top_in, acc_in, top, acc):
    def step(qi, carry):
        attend_chunks(flag_ref, 2, qi, q_ref, [up_ref, down_ref], top.at[qi], acc.at[qi])
        return carry

    lax.fori_loop(0, 4, step, 0)


def attend_last_kernel(blocks, flag_ref, q_ref, far0_ref, far1_ref, top_in, acc_in, *refs):
    outs, (top, acc) = refs[:-2], refs[-2:]
    for i, qi in enumerate(blocks):
        top[...] = top_in[qi]
        acc[...] = acc_in[qi]
        attend_chunks(flag_ref, 6, qi, q_ref, [far0_ref, far1_ref], top, acc)
        for h in range(H // KVH):
            outs[i][:, h * HD : (h + 1) * HD] = (acc[h, :, :HD] / acc[h, :, HD:]).astype(BF)


STATE = [
    jax.ShapeDtypeStruct((4, H // KVH, BLK, HD), F32),
    jax.ShapeDtypeStruct((4, H // KVH, BLK, 2 * HD), F32),
]


def attend_call(kernel, flags, arrays, outs, scratch=(), aliases=None, share=1, name="attend"):
    vm = pl.BlockSpec(memory_space=pltpu.VMEM)
    return pl.pallas_call(
        kernel,
        in_specs=[pl.BlockSpec(memory_space=pltpu.SMEM)] + [vm] * len(arrays),
        out_specs=[vm] * len(outs),
        out_shape=outs,
        scratch_shapes=list(scratch),
        input_output_aliases=aliases or {},
        compiler_params=pltpu.CompilerParams(vmem_limit_bytes=24 * 1024 * 1024),
        cost_estimate=pl.CostEstimate(flops=share << 30, bytes_accessed=4 << 20, transcendentals=share << 20),
        name=name,
    )(flags, *arrays)


def place_kernel(j_ref, *refs):
    out_ref = refs[-1]
    for k in range(4):
        cols = pl.ds(pl.multiple_of((j_ref[0] ^ k) * GW, GW), GW)
        out_ref[:, cols] = refs[k][...]


def place_call(j, parts):
    vm = pl.BlockSpec(memory_space=pltpu.VMEM)
    return pl.pallas_call(
        place_kernel,
        in_specs=[pl.BlockSpec(memory_space=pltpu.SMEM)] + [vm] * 4,
        out_specs=vm,
        out_shape=jax.ShapeDtypeStruct((BLK, H * HD), BF),
        compiler_params=pltpu.CompilerParams(vmem_limit_bytes=8 * 1024 * 1024),
        name="place",
    )(j, *parts)


def rotary_tables(start, count):
    half_dim = HD // 2
    positions = start + jnp.arange(count, dtype=jnp.int32)
    inv_freq = jnp.exp(jnp.arange(half_dim, dtype=F32) * (-2.0 * math.log(1000000.0) / HD))
    angle = positions.astype(F32)[:, None] * inv_freq[None, :]
    cosine, sine = jnp.cos(angle), jnp.sin(angle)
    return jnp.concatenate([cosine, cosine], 1), jnp.concatenate([-sine, sine], 1)


def on_device(hidden_in, queries, kv_weight, kv_bias, norm_gain, block_mask):
    f = lax.axis_index("fsdp")
    c = lax.axis_index("ctx")
    core, xi, yhi = f & 1, (f >> 1) & 3, f >> 3
    z, ylo = c & 7, c >> 3
    j = ylo * 2 + (z & 1)
    zq = z >> 1
    hidden = hidden_in.reshape(BLK, D)
    q = queries.reshape(BLK, H * HD)
    j1 = jnp.reshape(j, (1,))

    w_core = lax.ppermute(kv_weight, "fsdp", CORE_PAIRS)
    w_y = lax.ppermute(kv_weight, ("ctx", "fsdp"), DIAG_PAIRS)

    normed = norm_call(jnp.stack([xi, yhi, core]), hidden, norm_gain.reshape(1, D))
    n2 = lax.ppermute(normed[2], "fsdp", x_pairs(2))
    n1 = lax.ppermute(normed[1], "fsdp", x_pairs(1))
    n3 = lax.ppermute(normed[3], "fsdp", x_pairs(3))
    w_yc = lax.ppermute(w_y, "fsdp", CORE_PAIRS)

    q_parts = []
    for k in range(4):
        piece = lax.dynamic_slice(q, (0, (j ^ k) * GW), (BLK, GW))
        q_parts.append(piece if k == 0 else lax.ppermute(piece, "ctx", member_pairs(k)))
    q4 = jnp.stack(q_parts)

    weights = [kv_weight, w_core, w_y, w_yc]
    products = product_call([n1, n3, n2], weights, BF, "products")
    back = [lax.ppermute(p, "fsdp", x_pairs(k)) for p, k in zip(products, (3, 1, 2))]
    (own,) = product_call([normed[0]], weights, F32, "own_product")

    cos, sin = rotary_tables(c * BLK, BLK)
    kvs = kv_call(j1, own, back[0], back[1], back[2], kv_bias.reshape(1, -1), cos, sin)
    group = jnp.concatenate([kvs[0]] + [lax.ppermute(kvs[k], "ctx", member_pairs(k)) for k in (1, 2, 3)], axis=0)

    up = lax.ppermute(group, "ctx", z_pairs(2))
    down = lax.ppermute(group, "ctx", z_pairs(-2))
    far0 = lax.ppermute(up[:256], "ctx", z_pairs(2))
    far1 = lax.ppermute(down[256:], "ctx", z_pairs(-2))

    members = j ^ jnp.arange(4, dtype=jnp.int32)
    block_of = lambda at: (members >> 1) * 8 + 2 * at + (members & 1)
    q_ids = block_of(zq)
    u_ids = jnp.concatenate([q_ids, block_of((zq + 3) & 3), block_of((zq + 1) & 3), block_of((zq + 2) & 3)])
    table = block_mask.reshape(16, 16)
    seen = jnp.take(jnp.take(table, q_ids, axis=0), u_ids, axis=1) == 1
    order = q_ids[:, None] - u_ids[None, :]
    flags = jnp.where(order == 0, 2, jnp.where(order > 0, 1, 0)) * seen.astype(jnp.int32)

    flags = flags.astype(jnp.int32)

    top, acc = attend_call(attend_first_kernel, flags, [q4, group], STATE, share=1, name="attend_first")
    top, acc = attend_call(
        attend_more_kernel, flags, [q4, up, down, top, acc], STATE, aliases={4: 0, 5: 1}, share=3, name="attend_more"
    )

    def finish(blocks, name):
        return attend_call(
            lambda *refs: attend_last_kernel(blocks, *refs),
            flags,
            [q4, far0, far1, top, acc],
            [jax.ShapeDtypeStruct((BLK, GW), BF)] * len(blocks),
            scratch=[pltpu.VMEM(STATE[0].shape[1:], F32), pltpu.VMEM(STATE[1].shape[1:], F32)],
            name=name,
        )

    out3, out2 = finish((3, 2), "attend_others")
    out1, out0 = finish((1, 0), "attend_own")
    parts = [out0] + [lax.ppermute(o, "ctx", member_pairs(k)) for k, o in ((1, out1), (2, out2), (3, out3))]
    return place_call(j1, parts).reshape(1, BLK, H * HD)


def solution(mesh):
    return jax.shard_map(
        on_device,
        mesh=mesh,
        in_specs=(
            P("fsdp", "ctx", None),
            P("fsdp", "ctx", None),
            P("fsdp", None),
            P(),
            P(),
            P("fsdp", None, None),
        ),
        out_specs=P("fsdp", "ctx", None),
        check_vma=False,
    )
```

```python
import math

import jax
import jax.numpy as jnp
from jax import lax
from jax.experimental import pallas as pl
from jax.experimental.pallas import tpu as pltpu
from jax.sharding import PartitionSpec as P

H = 32
KVH = 4
HD = 128
BLK = 128
D = 8192
GW = (H // KVH) * HD
LOW = -1e30
SCALE = math.log2(math.e) / math.sqrt(HD)
BF = jnp.bfloat16
F32 = jnp.float32


def x_pairs(k):
    return [(f, (f & 8) | ((((f >> 1) + k) & 3) << 1) | (f & 1)) for f in range(16)]


CORE_PAIRS = [(f, f ^ 1) for f in range(16)]
DIAG_PAIRS = [(i, i ^ (8 * 16) ^ 8) for i in range(256)]


def member_pairs(k):
    flip = ((k >> 1) << 3) | (k & 1)
    return [(c, c ^ flip) for c in range(16)]


def z_pairs(k):
    return [(c, (c & 8) | ((c + k) & 7)) for c in range(16)]


def norm_kernel(pos_ref, x_hbm, gain_hbm, *refs):
    outs, (x_ref, gain_ref, sems) = refs[:4], refs[4:]
    xi, yhi, core = pos_ref[0], pos_ref[1], pos_ref[2]
    step = 32
    count = x_ref.shape[0] // step
    copies = [
        pltpu.make_async_copy(
            x_hbm.at[pl.ds(i * step, step)], x_ref.at[pl.ds(i * step, step)], sems.at[i]
        )
        for i in range(count)
    ]
    gain_copy = pltpu.make_async_copy(gain_hbm, gain_ref, sems.at[count])
    copies[0].start()
    gain_copy.start()
    for copy in copies[1:]:
        copy.start()
    for n in range(count):
        copies[n].wait()
        if n == 0:
            gain_copy.wait()
        rows = slice(n * step, (n + 1) * step)
        total = None
        for j in range(D // 128):
            part = x_ref[rows, j * 128 : (j + 1) * 128].astype(F32)
            part = part * part
            total = part if total is None else total + part
        inv = lax.rsqrt(jnp.sum(total, axis=-1, keepdims=True) / D + 1e-06)
        for k in (2, 1, 3, 0):
            for a in range(2):
                for b in range(2):
                    src = (yhi ^ a) * 4096 + ((xi + k) & 3) * 1024 + (core ^ b) * 512
                    cols = pl.ds(pl.multiple_of(src, 512), 512)
                    wide = x_ref[rows, cols].astype(F32)
                    dst = (a * 2 + b) * 512
                    outs[k][rows, dst : dst + 512] = (wide * inv * gain_ref[:, cols]).astype(BF)


def norm_call(pos, hidden, gain):
    rows = hidden.shape[0]
    vm = pl.BlockSpec(memory_space=pltpu.VMEM)
    hbm = pl.BlockSpec(memory_space=pl.ANY)
    return pl.pallas_call(
        norm_kernel,
        in_specs=[pl.BlockSpec(memory_space=pltpu.SMEM), hbm, hbm],
        out_specs=[vm] * 4,
        out_shape=[jax.ShapeDtypeStruct((rows, D // 4), BF)] * 4,
        scratch_shapes=[
            pltpu.VMEM((rows, D), BF),
            pltpu.VMEM((1, D), F32),
            pltpu.SemaphoreType.DMA((rows // 32 + 1,)),
        ],
        compiler_params=pltpu.CompilerParams(vmem_limit_bytes=50 * 1024 * 1024),
        cost_estimate=pl.CostEstimate(flops=4 << 20, bytes_accessed=4 << 20, transcendentals=0),
        name="norm",
    )(pos, hidden, gain)


def product_kernel(count, *refs):
    rows, weights, outs = refs[:count], refs[count : -count], refs[-count:]
    tokens = rows[0].shape[0]
    for n in range(4):
        cols = slice(n * 256, (n + 1) * 256)
        left = jnp.concatenate([r[...] for r in rows], axis=0)
        right = jnp.concatenate([w[:, cols] for w in weights], axis=0)
        total = jnp.dot(left, right, preferred_element_type=F32)
        for i in range(count):
            outs[i][:, cols] = total[i * tokens : (i + 1) * tokens].astype(outs[i].dtype)


def product_call(rows, weights, dtype, name):
    vm = pl.BlockSpec(memory_space=pltpu.VMEM)
    count, tokens = len(rows), rows[0].shape[0]
    return pl.pallas_call(
        lambda *refs: product_kernel(count, *refs),
        in_specs=[vm] * (count + len(weights)),
        out_specs=[vm] * count,
        out_shape=[jax.ShapeDtypeStruct((tokens, 1024), dtype)] * count,
        compiler_params=pltpu.CompilerParams(vmem_limit_bytes=24 * 1024 * 1024),
        cost_estimate=pl.CostEstimate(
            flops=count * tokens * 2048 * 2048, bytes_accessed=4 << 20, transcendentals=0
        ),
        name=name,
    )(*rows, *weights)


def kv_kernel(j_ref, own_ref, r1_ref, r2_ref, r3_ref, bias_ref, cos_ref, sin_ref, *outs):
    j = j_ref[0]

    def part(col):
        cols = pl.ds(pl.multiple_of(col, 128), 128)
        back = r1_ref[:, cols].astype(F32) + r2_ref[:, cols].astype(F32) + r3_ref[:, cols].astype(F32)
        return own_ref[:, cols] + back + bias_ref[:, cols]

    for k in range(4):
        head = j ^ k
        key = part(head * HD)
        turned = key * cos_ref[...] + pltpu.roll(key, HD // 2, 1) * sin_ref[...]
        outs[k][:, :HD] = turned.astype(BF)
        outs[k][:, HD:] = part(KVH * HD + head * HD).astype(BF)


def kv_call(j, own, r1, r2, r3, bias, cos, sin):
    vm = pl.BlockSpec(memory_space=pltpu.VMEM)
    return pl.pallas_call(
        kv_kernel,
        in_specs=[pl.BlockSpec(memory_space=pltpu.SMEM)] + [vm] * 7,
        out_specs=[vm] * 4,
        out_shape=[jax.ShapeDtypeStruct((own.shape[0], 2 * HD), BF)] * 4,
        compiler_params=pltpu.CompilerParams(vmem_limit_bytes=8 * 1024 * 1024),
        cost_estimate=pl.CostEstimate(flops=1 << 20, bytes_accessed=2 << 20, transcendentals=0),
        name="keys_values",
    )(j, own, r1, r2, r3, bias, cos, sin)


def visit(pair, q_ref, pieces, reach, top, acc, fresh=False):
    parts = [ref[pl.ds(row, 256), :] for ref, row in pieces]
    width = 256 * len(parts)
    keys = jnp.concatenate([p[:, :HD] for p in parts], axis=0)
    values = jnp.concatenate([p[:, HD:] for p in parts], axis=0)
    values = jnp.concatenate([values, jnp.ones((width, HD), BF)], axis=1)
    for b in range(2):
        block = pair * 2 + b
        for h in range(0, H // KVH, 4):
            q = jnp.concatenate([q_ref[block, :, (h + i) * HD : (h + i + 1) * HD] for i in range(4)], axis=0)
            s = lax.dot_general(q, keys, (((1,), (1,)), ((), ())), preferred_element_type=F32)
            if reach is not None:
                col = lax.broadcasted_iota(jnp.int32, (BLK, BLK), 1)
                valid = jnp.concatenate([col <= r for r in reach[b]], axis=1)
                s = jnp.where(jnp.concatenate([valid] * 4, axis=0), s, LOW)
            rows = slice(h * BLK, (h + 4) * BLK)
            peak = jnp.max(s, axis=-1, keepdims=True)
            if fresh:
                new = jnp.broadcast_to(peak, (4 * BLK, HD))
            else:
                old = top[block, rows]
                new = jnp.maximum(old, peak)
            top[block, rows] = new
            shift = new if reach is None else jnp.maximum(new, LOW / 2)
            p = jnp.exp2((s - jnp.concatenate([shift] * (width // HD), axis=1)) * SCALE)
            add = jnp.dot(p.astype(BF), values, preferred_element_type=F32)
            if fresh:
                acc[block, rows] = add
            else:
                factor = jnp.exp2((old - new) * SCALE)
                acc[block, rows] = acc[block, rows] * jnp.concatenate([factor, factor], axis=1) + add


def reaches(flag_ref, pair, blocks):
    row = lax.broadcasted_iota(jnp.int32, (BLK, BLK), 0)
    out = []
    for b in range(2):
        flags = [flag_ref[pair * 2 + b, u] for u in blocks]
        out.append([jnp.where(f == 2, row, jnp.where(f == 1, BLK, -1)) for f in flags])
    return out


def flag_sum(flag_ref, pair, blocks):
    return sum(flag_ref[pair * 2 + b, u] for b in range(2) for u in blocks)


def all_whole(flag_ref, pair, blocks):
    whole = True
    for b in range(2):
        for u in blocks:
            whole = (flag_ref[pair * 2 + b, u] == 1) & whole
    return whole


def attend_source(flag_ref, source, pair, q_ref, pieces, top, acc):
    blocks = [source * 4 + i for i in range(4)]
    whole = all_whole(flag_ref, pair, blocks)

    @pl.when(whole)
    def _():
        visit(pair, q_ref, pieces, None, top, acc)

    for i in range(2):
        half = blocks[2 * i : 2 * i + 2]

        @pl.when(jnp.logical_not(whole) & (flag_sum(flag_ref, pair, half) > 0))
        def _(i=i, half=half):
            visit(pair, q_ref, pieces[i : i + 1], reaches(flag_ref, pair, half), top, acc)


def attend_first_kernel(flag_ref, q_ref, kv_ref, top, acc):
    def step(pair, carry):
        other = flag_sum(flag_ref, pair, [(1 - pair) * 2, (1 - pair) * 2 + 1])
        both = other > 0

        @pl.when(both)
        def _():
            visit(pair, q_ref, [(kv_ref, 0), (kv_ref, 256)], reaches(flag_ref, pair, range(4)), top, acc, True)

        @pl.when(jnp.logical_not(both))
        def _():
            row = pl.multiple_of(pair * 256, 256)
            mine = [pair * 2, pair * 2 + 1]
            visit(pair, q_ref, [(kv_ref, row)], reaches(flag_ref, pair, mine), top, acc, True)

        return carry

    lax.fori_loop(0, 2, step, 0)


def attend_more_kernel(flag_ref, q_ref, up_ref, down_ref, top_in, acc_in, top, acc):
    def step(pair, carry):
        for source, ref in ((1, up_ref), (2, down_ref)):
            attend_source(flag_ref, source, pair, q_ref, [(ref, 0), (ref, 256)], top, acc)
        return carry

    lax.fori_loop(0, 2, step, 0)


def attend_last_kernel(pair, flag_ref, q_ref, far0_ref, far1_ref, top_in, acc_in, top, acc, *outs):
    attend_source(flag_ref, 3, pair, q_ref, [(far0_ref, 0), (far1_ref, 0)], top, acc)
    for b in range(2):
        for h in range(H // KVH):
            rows = slice(h * BLK, (h + 1) * BLK)
            mixed = acc[pair * 2 + b, rows]
            outs[b][:, h * HD : (h + 1) * HD] = (mixed[:, :HD] / mixed[:, HD:]).astype(BF)


STATE = [
    jax.ShapeDtypeStruct((4, GW, HD), F32),
    jax.ShapeDtypeStruct((4, GW, 2 * HD), F32),
]


def attend_call(kernel, flags, arrays, outs, aliases=None, share=1, name="attend"):
    vm = pl.BlockSpec(memory_space=pltpu.VMEM)
    return pl.pallas_call(
        kernel,
        in_specs=[pl.BlockSpec(memory_space=pltpu.SMEM)] + [vm] * len(arrays),
        out_specs=[vm] * len(outs),
        out_shape=outs,
        input_output_aliases=aliases or {},
        compiler_params=pltpu.CompilerParams(vmem_limit_bytes=24 * 1024 * 1024),
        cost_estimate=pl.CostEstimate(flops=share << 30, bytes_accessed=4 << 20, transcendentals=share << 20),
        name=name,
    )(flags, *arrays)


def place_kernel(j_ref, *refs):
    out_ref = refs[-1]
    for k in range(4):
        cols = pl.ds(pl.multiple_of((j_ref[0] ^ k) * GW, GW), GW)
        out_ref[:, cols] = refs[k][...]


def place_call(j, parts):
    vm = pl.BlockSpec(memory_space=pltpu.VMEM)
    return pl.pallas_call(
        place_kernel,
        in_specs=[pl.BlockSpec(memory_space=pltpu.SMEM)] + [vm] * 4,
        out_specs=vm,
        out_shape=jax.ShapeDtypeStruct((BLK, H * HD), BF),
        compiler_params=pltpu.CompilerParams(vmem_limit_bytes=8 * 1024 * 1024),
        name="place",
    )(j, *parts)


def rotary_tables(start, count):
    half_dim = HD // 2
    positions = start + jnp.arange(count, dtype=jnp.int32)
    inv_freq = jnp.exp(jnp.arange(half_dim, dtype=F32) * (-2.0 * math.log(1000000.0) / HD))
    angle = positions.astype(F32)[:, None] * inv_freq[None, :]
    cosine, sine = jnp.cos(angle), jnp.sin(angle)
    return jnp.concatenate([cosine, cosine], 1), jnp.concatenate([-sine, sine], 1)


def on_device(hidden_in, queries, kv_weight, kv_bias, norm_gain, block_mask):
    f = lax.axis_index("fsdp")
    c = lax.axis_index("ctx")
    core, xi, yhi = f & 1, (f >> 1) & 3, f >> 3
    z, ylo = c & 7, c >> 3
    j = ylo * 2 + (z & 1)
    zq = z >> 1
    hidden = hidden_in.reshape(BLK, D)
    q = queries.reshape(BLK, H * HD)
    j1 = jnp.reshape(j, (1,))

    w_core = lax.ppermute(kv_weight, "fsdp", CORE_PAIRS)
    w_y = lax.ppermute(kv_weight, ("ctx", "fsdp"), DIAG_PAIRS)

    normed = norm_call(jnp.stack([xi, yhi, core]), hidden, norm_gain.reshape(1, D))
    n2 = lax.ppermute(normed[2], "fsdp", x_pairs(2))
    n1 = lax.ppermute(normed[1], "fsdp", x_pairs(1))
    n3 = lax.ppermute(normed[3], "fsdp", x_pairs(3))
    w_yc = lax.ppermute(w_y, "fsdp", CORE_PAIRS)

    q_parts = []
    for k in range(4):
        piece = lax.dynamic_slice(q, (0, (j ^ k) * GW), (BLK, GW))
        q_parts.append(piece if k == 0 else lax.ppermute(piece, "ctx", member_pairs(k)))
    q4 = jnp.stack(q_parts)

    weights = [kv_weight, w_core, w_y, w_yc]
    products = product_call([n1, n3, n2], weights, BF, "products")
    back = [lax.ppermute(p, "fsdp", x_pairs(k)) for p, k in zip(products, (3, 1, 2))]
    (own,) = product_call([normed[0]], weights, F32, "own_product")

    cos, sin = rotary_tables(c * BLK, BLK)
    kvs = kv_call(j1, own, back[0], back[1], back[2], kv_bias.reshape(1, -1), cos, sin)
    group = jnp.concatenate([kvs[0]] + [lax.ppermute(kvs[k], "ctx", member_pairs(k)) for k in (1, 2, 3)], axis=0)

    up = lax.ppermute(group, "ctx", z_pairs(2))
    down = lax.ppermute(group, "ctx", z_pairs(-2))
    far0 = lax.ppermute(up[:256], "ctx", z_pairs(2))
    far1 = lax.ppermute(down[256:], "ctx", z_pairs(-2))

    members = j ^ jnp.arange(4, dtype=jnp.int32)
    block_of = lambda at: (members >> 1) * 8 + 2 * at + (members & 1)
    q_ids = block_of(zq)
    u_ids = jnp.concatenate([q_ids, block_of((zq + 3) & 3), block_of((zq + 1) & 3), block_of((zq + 2) & 3)])
    table = block_mask.reshape(16, 16)
    seen = jnp.take(jnp.take(table, q_ids, axis=0), u_ids, axis=1) == 1
    order = q_ids[:, None] - u_ids[None, :]
    flags = jnp.where(order == 0, 2, jnp.where(order > 0, 1, 0)) * seen.astype(jnp.int32)

    flags = flags.astype(jnp.int32)

    top, acc = attend_call(attend_first_kernel, flags, [q4, group], STATE, share=1, name="attend_first")
    top, acc = attend_call(
        attend_more_kernel, flags, [q4, up, down, top, acc], STATE, aliases={4: 0, 5: 1}, share=3, name="attend_more"
    )

    def finish(pair, top, acc, name):
        return attend_call(
            lambda *refs: attend_last_kernel(pair, *refs),
            flags,
            [q4, far0, far1, top, acc],
            STATE + [jax.ShapeDtypeStruct((BLK, GW), BF)] * 2,
            aliases={4: 0, 5: 1},
            name=name,
        )

    top, acc, out2, out3 = finish(1, top, acc, "attend_others")
    top, acc, out0, out1 = finish(0, top, acc, "attend_own")
    parts = [out0] + [lax.ppermute(o, "ctx", member_pairs(k)) for k, o in ((1, out1), (2, out2), (3, out3))]
    return place_call(j1, parts).reshape(1, BLK, H * HD)


def solution(mesh):
    return jax.shard_map(
        on_device,
        mesh=mesh,
        in_specs=(
            P("fsdp", "ctx", None),
            P("fsdp", "ctx", None),
            P("fsdp", None),
            P(),
            P(),
            P("fsdp", None, None),
        ),
        out_specs=P("fsdp", "ctx", None),
        check_vma=False,
    )
```

```python
import math

import jax
import jax.numpy as jnp
from jax import lax
from jax.experimental import pallas as pl
from jax.experimental.pallas import tpu as pltpu
from jax.sharding import PartitionSpec as P

H = 32
KVH = 4
HD = 128
BLK = 128
D = 8192
GW = (H // KVH) * HD
LOW = -1e30
SCALE = math.log2(math.e) / math.sqrt(HD)
BF = jnp.bfloat16
F32 = jnp.float32


def x_pairs(k):
    return [(f, (f & 8) | ((((f >> 1) + k) & 3) << 1) | (f & 1)) for f in range(16)]


CORE_PAIRS = [(f, f ^ 1) for f in range(16)]
DIAG_PAIRS = [(i, i ^ (8 * 16) ^ 8) for i in range(256)]


def member_pairs(k):
    flip = ((k >> 1) << 3) | (k & 1)
    return [(c, c ^ flip) for c in range(16)]


def z_pairs(k):
    return [(c, (c & 8) | ((c + k) & 7)) for c in range(16)]


def part_column(pos_ref, k, i):
    a, b = i >> 1, i & 1
    src = (pos_ref[1] ^ a) * 4096 + ((pos_ref[0] + k) & 3) * 1024 + (pos_ref[2] ^ b) * 512
    return pl.multiple_of(src, 512)


def norm_kernel(pos_ref, x_hbm, gain_hbm, out0, out1, out2, out3, x_ref, gain_ref, sems):
    step = 32
    count = x_ref.shape[0] // step
    copies = [
        pltpu.make_async_copy(
            x_hbm.at[pl.ds(i * step, step)], x_ref.at[pl.ds(i * step, step)], sems.at[i]
        )
        for i in range(count)
    ]
    gain_copy = pltpu.make_async_copy(gain_hbm, gain_ref, sems.at[count])
    copies[0].start()
    gain_copy.start()
    for copy in copies[1:]:
        copy.start()
    for n in range(count):
        copies[n].wait()
        if n == 0:
            gain_copy.wait()
        rows = slice(n * step, (n + 1) * step)
        total = None
        for j in range(D // 128):
            part = x_ref[rows, j * 128 : (j + 1) * 128].astype(F32)
            part = part * part
            total = part if total is None else total + part
        inv = lax.rsqrt(jnp.sum(total, axis=-1, keepdims=True) / D + 1e-06)
        for k, out in ((2, out2), (1, out1), (3, out3), (0, out0)):
            for i in range(4):
                cols = pl.ds(part_column(pos_ref, k, i), 512)
                wide = x_ref[rows, cols].astype(F32)
                out[rows, i * 512 : (i + 1) * 512] = (wide * inv * gain_ref[:, cols]).astype(BF)


def norm_call(pos, hidden, gain):
    rows = hidden.shape[0]
    vm = pl.BlockSpec(memory_space=pltpu.VMEM)
    hbm = pl.BlockSpec(memory_space=pl.ANY)
    return pl.pallas_call(
        norm_kernel,
        in_specs=[pl.BlockSpec(memory_space=pltpu.SMEM), hbm, hbm],
        out_specs=[vm] * 4,
        out_shape=[jax.ShapeDtypeStruct((rows, D // 4), BF)] * 4,
        scratch_shapes=[
            pltpu.VMEM((rows, D), BF),
            pltpu.VMEM((1, D), F32),
            pltpu.SemaphoreType.DMA((rows // 32 + 1,)),
        ],
        compiler_params=pltpu.CompilerParams(vmem_limit_bytes=50 * 1024 * 1024),
        cost_estimate=pl.CostEstimate(flops=4 << 20, bytes_accessed=4 << 20, transcendentals=0),
        name="norm",
    )(pos, hidden, gain)


def product_kernel(count, *refs):
    rows, weights, outs = refs[:count], refs[count:-count], refs[-count:]
    tokens = rows[0].shape[0]
    left = jnp.concatenate([r[...] for r in rows], axis=0)
    right = jnp.concatenate([w[...] for w in weights], axis=0)
    total = jnp.dot(left, right, preferred_element_type=F32)
    for i in range(count):
        outs[i][...] = total[i * tokens : (i + 1) * tokens].astype(outs[i].dtype)


def product_call(rows, weights, dtype, name):
    vm = pl.BlockSpec(memory_space=pltpu.VMEM)
    count, tokens = len(rows), rows[0].shape[0]
    return pl.pallas_call(
        lambda *refs: product_kernel(count, *refs),
        in_specs=[vm] * (count + len(weights)),
        out_specs=[vm] * count,
        out_shape=[jax.ShapeDtypeStruct((tokens, 1024), dtype)] * count,
        compiler_params=pltpu.CompilerParams(vmem_limit_bytes=24 * 1024 * 1024),
        cost_estimate=pl.CostEstimate(
            flops=count * tokens * 2048 * 2048, bytes_accessed=4 << 20, transcendentals=0
        ),
        name=name,
    )(*rows, *weights)


def kv_kernel(j_ref, own_ref, r1_ref, r3_ref, r2_ref, bias_ref, cos_ref, sin_ref, *outs):
    j = j_ref[0]

    def part(col):
        cols = pl.ds(pl.multiple_of(col, 128), 128)
        back = r1_ref[:, cols].astype(F32) + r3_ref[:, cols].astype(F32) + r2_ref[:, cols].astype(F32)
        return own_ref[:, cols] + back + bias_ref[:, cols]

    for k in range(4):
        head = j ^ k
        key = part(head * HD)
        turned = key * cos_ref[...] + pltpu.roll(key, HD // 2, 1) * sin_ref[...]
        outs[k][:, :HD] = turned.astype(BF)
        outs[k][:, HD:] = part(KVH * HD + head * HD).astype(BF)


def kv_call(j, own, r1, r3, r2, bias, cos, sin):
    vm = pl.BlockSpec(memory_space=pltpu.VMEM)
    return pl.pallas_call(
        kv_kernel,
        in_specs=[pl.BlockSpec(memory_space=pltpu.SMEM)] + [vm] * 7,
        out_specs=[vm] * 4,
        out_shape=[jax.ShapeDtypeStruct((own.shape[0], 2 * HD), BF)] * 4,
        compiler_params=pltpu.CompilerParams(vmem_limit_bytes=8 * 1024 * 1024),
        cost_estimate=pl.CostEstimate(flops=1 << 20, bytes_accessed=2 << 20, transcendentals=0),
        name="keys_values",
    )(j, own, r1, r3, r2, bias, cos, sin)


def visit(pair, q_ref, pieces, reach, top, acc, fresh=False):
    parts = [ref[pl.ds(row, 256), :] for ref, row in pieces]
    width = 256 * len(parts)
    keys = jnp.concatenate([p[:, :HD] for p in parts], axis=0)
    values = jnp.concatenate([p[:, HD:] for p in parts], axis=0)
    values = jnp.concatenate([values, jnp.ones((width, HD), BF)], axis=1)
    for b in range(2):
        block = pair * 2 + b
        for h in range(0, H // KVH, 4):
            q = jnp.concatenate([q_ref[block, :, (h + i) * HD : (h + i + 1) * HD] for i in range(4)], axis=0)
            s = lax.dot_general(q, keys, (((1,), (1,)), ((), ())), preferred_element_type=F32)
            if reach is not None:
                col = lax.broadcasted_iota(jnp.int32, (BLK, BLK), 1)
                valid = jnp.concatenate([col <= r for r in reach[b]], axis=1)
                s = jnp.where(jnp.concatenate([valid] * 4, axis=0), s, LOW)
            rows = slice(h * BLK, (h + 4) * BLK)
            peak = jnp.max(s, axis=-1, keepdims=True)
            if fresh:
                new = jnp.broadcast_to(peak, (4 * BLK, HD))
            else:
                old = top[block, rows]
                new = jnp.maximum(old, peak)
            top[block, rows] = new
            shift = new if reach is None else jnp.maximum(new, LOW / 2)
            p = jnp.exp2((s - jnp.concatenate([shift] * (width // HD), axis=1)) * SCALE)
            add = jnp.dot(p.astype(BF), values, preferred_element_type=F32)
            if fresh:
                acc[block, rows] = add
            else:
                factor = jnp.exp2((old - new) * SCALE)
                acc[block, rows] = acc[block, rows] * jnp.concatenate([factor, factor], axis=1) + add


def reaches(flag_ref, pair, blocks):
    row = lax.broadcasted_iota(jnp.int32, (BLK, BLK), 0)
    out = []
    for b in range(2):
        flags = [flag_ref[pair * 2 + b, u] for u in blocks]
        out.append([jnp.where(f == 2, row, jnp.where(f == 1, BLK, -1)) for f in flags])
    return out


def flag_sum(flag_ref, pair, blocks):
    return sum(flag_ref[pair * 2 + b, u] for b in range(2) for u in blocks)


def all_whole(flag_ref, pair, blocks):
    whole = True
    for b in range(2):
        for u in blocks:
            whole = (flag_ref[pair * 2 + b, u] == 1) & whole
    return whole


def attend_source(flag_ref, source, pair, q_ref, pieces, top, acc):
    blocks = [source * 4 + i for i in range(4)]
    whole = all_whole(flag_ref, pair, blocks)

    @pl.when(whole)
    def _():
        visit(pair, q_ref, pieces, None, top, acc)

    for i in range(2):
        half = blocks[2 * i : 2 * i + 2]

        @pl.when(jnp.logical_not(whole) & (flag_sum(flag_ref, pair, half) > 0))
        def _(i=i, half=half):
            visit(pair, q_ref, pieces[i : i + 1], reaches(flag_ref, pair, half), top, acc)


def attend_first_kernel(flag_ref, q_ref, kv_ref, top, acc):
    def step(pair, carry):
        other = flag_sum(flag_ref, pair, [(1 - pair) * 2, (1 - pair) * 2 + 1])
        both = other > 0

        @pl.when(both)
        def _():
            visit(pair, q_ref, [(kv_ref, 0), (kv_ref, 256)], reaches(flag_ref, pair, range(4)), top, acc, True)

        @pl.when(jnp.logical_not(both))
        def _():
            row = pl.multiple_of(pair * 256, 256)
            mine = [pair * 2, pair * 2 + 1]
            visit(pair, q_ref, [(kv_ref, row)], reaches(flag_ref, pair, mine), top, acc, True)

        return carry

    lax.fori_loop(0, 2, step, 0)


def attend_more_kernel(flag_ref, q_ref, up_ref, down_ref, top_in, acc_in, top, acc):
    def step(pair, carry):
        for source, ref in ((1, up_ref), (2, down_ref)):
            attend_source(flag_ref, source, pair, q_ref, [(ref, 0), (ref, 256)], top, acc)
        return carry

    lax.fori_loop(0, 2, step, 0)


def attend_last_kernel(pair, flag_ref, q_ref, far0_ref, far1_ref, top_in, acc_in, top, acc, *outs):
    attend_source(flag_ref, 3, pair, q_ref, [(far0_ref, 0), (far1_ref, 0)], top, acc)
    for b in range(2):
        for h in range(H // KVH):
            rows = slice(h * BLK, (h + 1) * BLK)
            mixed = acc[pair * 2 + b, rows]
            outs[b][:, h * HD : (h + 1) * HD] = (mixed[:, :HD] / mixed[:, HD:]).astype(BF)


STATE = [
    jax.ShapeDtypeStruct((4, GW, HD), F32),
    jax.ShapeDtypeStruct((4, GW, 2 * HD), F32),
]


def attend_call(kernel, flags, arrays, outs, aliases=None, share=1, name="attend"):
    vm = pl.BlockSpec(memory_space=pltpu.VMEM)
    return pl.pallas_call(
        kernel,
        in_specs=[pl.BlockSpec(memory_space=pltpu.SMEM)] + [vm] * len(arrays),
        out_specs=[vm] * len(outs),
        out_shape=outs,
        input_output_aliases=aliases or {},
        compiler_params=pltpu.CompilerParams(vmem_limit_bytes=24 * 1024 * 1024),
        cost_estimate=pl.CostEstimate(flops=share << 30, bytes_accessed=4 << 20, transcendentals=share << 20),
        name=name,
    )(flags, *arrays)


def place_kernel(j_ref, *refs):
    out_ref = refs[-1]
    for k in range(4):
        cols = pl.ds(pl.multiple_of((j_ref[0] ^ k) * GW, GW), GW)
        out_ref[:, cols] = refs[k][...]


def place_call(j, parts):
    vm = pl.BlockSpec(memory_space=pltpu.VMEM)
    return pl.pallas_call(
        place_kernel,
        in_specs=[pl.BlockSpec(memory_space=pltpu.SMEM)] + [vm] * 4,
        out_specs=vm,
        out_shape=jax.ShapeDtypeStruct((BLK, H * HD), BF),
        compiler_params=pltpu.CompilerParams(vmem_limit_bytes=8 * 1024 * 1024),
        name="place",
    )(j, *parts)


def rotary_tables(start, count):
    half_dim = HD // 2
    positions = start + jnp.arange(count, dtype=jnp.int32)
    inv_freq = jnp.exp(jnp.arange(half_dim, dtype=F32) * (-2.0 * math.log(1000000.0) / HD))
    angle = positions.astype(F32)[:, None] * inv_freq[None, :]
    cosine, sine = jnp.cos(angle), jnp.sin(angle)
    return jnp.concatenate([cosine, cosine], 1), jnp.concatenate([-sine, sine], 1)


def after(value, earlier):
    return lax.optimization_barrier((value, earlier))[0]


def on_device(hidden_in, queries, kv_weight, kv_bias, norm_gain, block_mask):
    f = lax.axis_index("fsdp")
    c = lax.axis_index("ctx")
    core, xi, yhi = f & 1, (f >> 1) & 3, f >> 3
    z, ylo = c & 7, c >> 3
    j = ylo * 2 + (z & 1)
    zq = z >> 1
    hidden = hidden_in.reshape(BLK, D)
    q = queries.reshape(BLK, H * HD)
    j1 = jnp.reshape(j, (1,))

    pos = jnp.stack([xi, yhi, core])
    gain = norm_gain.reshape(1, D)
    w_y = lax.ppermute(kv_weight, ("ctx", "fsdp"), DIAG_PAIRS)

    normed0, normed1, normed2, normed3 = norm_call(pos, hidden, gain)
    n2 = lax.ppermute(normed2, "fsdp", x_pairs(2))
    n1 = lax.ppermute(normed1, "fsdp", x_pairs(1))
    n3 = lax.ppermute(normed3, "fsdp", x_pairs(3))
    q_parts = [lax.dynamic_slice(q, (0, (j ^ k) * GW), (BLK, GW)) for k in range(4)]
    q_parts[2] = lax.ppermute(after(q_parts[2], normed0), "ctx", member_pairs(2))
    q_parts[3] = lax.ppermute(after(q_parts[3], q_parts[2]), "ctx", member_pairs(3))
    w_core = lax.ppermute(after(kv_weight, q_parts[3]), "fsdp", CORE_PAIRS)
    w_yc = lax.ppermute(after(w_y, q_parts[3]), "fsdp", CORE_PAIRS)
    q_parts[1] = lax.ppermute(after(q_parts[1], w_core), "ctx", member_pairs(1))
    q4 = jnp.stack(q_parts)

    weights = [kv_weight, w_core, w_y, w_yc]
    p1, p3 = product_call([n1, n3], weights, BF, "products")
    (p2,) = product_call([n2], weights, BF, "far_product")
    back = [lax.ppermute(p, "fsdp", x_pairs(k)) for p, k in ((p1, 3), (p3, 1), (p2, 2))]
    (own,) = product_call([normed0], weights, F32, "own_product")

    cos, sin = rotary_tables(c * BLK, BLK)
    kvs = kv_call(j1, own, back[0], back[1], back[2], kv_bias.reshape(1, -1), cos, sin)
    group = jnp.concatenate([kvs[0]] + [lax.ppermute(kvs[k], "ctx", member_pairs(k)) for k in (1, 2, 3)], axis=0)

    up = lax.ppermute(group, "ctx", z_pairs(2))
    down = lax.ppermute(group, "ctx", z_pairs(-2))
    far0 = lax.ppermute(up[:256], "ctx", z_pairs(2))
    far1 = lax.ppermute(down[256:], "ctx", z_pairs(-2))

    members = j ^ jnp.arange(4, dtype=jnp.int32)
    block_of = lambda at: (members >> 1) * 8 + 2 * at + (members & 1)
    q_ids = block_of(zq)
    u_ids = jnp.concatenate([q_ids, block_of((zq + 3) & 3), block_of((zq + 1) & 3), block_of((zq + 2) & 3)])
    table = block_mask.reshape(16, 16)
    seen = jnp.take(jnp.take(table, q_ids, axis=0), u_ids, axis=1) == 1
    order = q_ids[:, None] - u_ids[None, :]
    flags = jnp.where(order == 0, 2, jnp.where(order > 0, 1, 0)) * seen.astype(jnp.int32)

    flags = flags.astype(jnp.int32)

    top, acc = attend_call(attend_first_kernel, flags, [q4, group], STATE, share=1, name="attend_first")
    top, acc = attend_call(
        attend_more_kernel, flags, [q4, up, down, top, acc], STATE, aliases={4: 0, 5: 1}, share=3, name="attend_more"
    )

    def finish(pair, top, acc, name):
        return attend_call(
            lambda *refs: attend_last_kernel(pair, *refs),
            flags,
            [q4, far0, far1, top, acc],
            STATE + [jax.ShapeDtypeStruct((BLK, GW), BF)] * 2,
            aliases={4: 0, 5: 1},
            name=name,
        )

    top, acc, out2, out3 = finish(1, top, acc, "attend_others")
    top, acc, out0, out1 = finish(0, top, acc, "attend_own")
    parts = [out0] + [lax.ppermute(o, "ctx", member_pairs(k)) for k, o in ((1, out1), (2, out2), (3, out3))]
    return place_call(j1, parts).reshape(1, BLK, H * HD)


def solution(mesh):
    return jax.shard_map(
        on_device,
        mesh=mesh,
        in_specs=(
            P("fsdp", "ctx", None),
            P("fsdp", "ctx", None),
            P("fsdp", None),
            P(),
            P(),
            P("fsdp", None, None),
        ),
        out_specs=P("fsdp", "ctx", None),
        check_vma=False,
    )
```

```python
import math

import jax
import jax.numpy as jnp
from jax import lax
from jax.experimental import pallas as pl
from jax.experimental.pallas import tpu as pltpu
from jax.sharding import PartitionSpec as P

H = 32
KVH = 4
HD = 128
BLK = 128
D = 8192
GW = (H // KVH) * HD
LOW = -1e30
SCALE = math.log2(math.e) / math.sqrt(HD)
BF = jnp.bfloat16
F32 = jnp.float32


def x_pairs(k):
    return [(f, (f & 8) | ((((f >> 1) + k) & 3) << 1) | (f & 1)) for f in range(16)]


CORE_PAIRS = [(f, f ^ 1) for f in range(16)]
DIAG_PAIRS = [(i, i ^ (8 * 16) ^ 8) for i in range(256)]


def member_pairs(k):
    flip = ((k >> 1) << 3) | (k & 1)
    return [(c, c ^ flip) for c in range(16)]


def z_pairs(k):
    return [(c, (c & 8) | ((c + k) & 7)) for c in range(16)]


def part_column(pos_ref, k, i):
    a, b = i >> 1, i & 1
    src = (pos_ref[1] ^ a) * 4096 + ((pos_ref[0] + k) & 3) * 1024 + (pos_ref[2] ^ b) * 512
    return pl.multiple_of(src, 512)


def norm_kernel(pos_ref, x_hbm, gain_hbm, out0, out1, out2, out3, x_ref, gain_ref, sems):
    step = 32
    count = x_ref.shape[0] // step
    copies = [
        pltpu.make_async_copy(
            x_hbm.at[pl.ds(i * step, step)], x_ref.at[pl.ds(i * step, step)], sems.at[i]
        )
        for i in range(count)
    ]
    gain_copy = pltpu.make_async_copy(gain_hbm, gain_ref, sems.at[count])
    copies[0].start()
    gain_copy.start()
    for copy in copies[1:]:
        copy.start()
    for n in range(count):
        copies[n].wait()
        if n == 0:
            gain_copy.wait()
        rows = slice(n * step, (n + 1) * step)
        total = None
        for j in range(D // 128):
            part = x_ref[rows, j * 128 : (j + 1) * 128].astype(F32)
            part = part * part
            total = part if total is None else total + part
        inv = lax.rsqrt(jnp.sum(total, axis=-1, keepdims=True) / D + 1e-06)
        for k, out in ((2, out2), (1, out1), (3, out3), (0, out0)):
            for i in range(4):
                cols = pl.ds(part_column(pos_ref, k, i), 512)
                wide = x_ref[rows, cols].astype(F32)
                out[rows, i * 512 : (i + 1) * 512] = (wide * inv * gain_ref[:, cols]).astype(BF)


def norm_call(pos, hidden, gain):
    rows = hidden.shape[0]
    vm = pl.BlockSpec(memory_space=pltpu.VMEM)
    hbm = pl.BlockSpec(memory_space=pl.ANY)
    return pl.pallas_call(
        norm_kernel,
        in_specs=[pl.BlockSpec(memory_space=pltpu.SMEM), hbm, hbm],
        out_specs=[vm] * 4,
        out_shape=[jax.ShapeDtypeStruct((rows, D // 4), BF)] * 4,
        scratch_shapes=[
            pltpu.VMEM((rows, D), BF),
            pltpu.VMEM((1, D), F32),
            pltpu.SemaphoreType.DMA((rows // 32 + 1,)),
        ],
        compiler_params=pltpu.CompilerParams(vmem_limit_bytes=50 * 1024 * 1024),
        cost_estimate=pl.CostEstimate(flops=4 << 20, bytes_accessed=4 << 20, transcendentals=0),
        name="norm",
    )(pos, hidden, gain)


def product_kernel(count, *refs):
    rows, weights, outs = refs[:count], refs[count:-count], refs[-count:]
    tokens = rows[0].shape[0]
    left = jnp.concatenate([r[...] for r in rows], axis=0)
    right = jnp.concatenate([w[...] for w in weights], axis=0)
    total = jnp.dot(left, right, preferred_element_type=F32)
    for i in range(count):
        outs[i][...] = total[i * tokens : (i + 1) * tokens].astype(outs[i].dtype)


def product_call(rows, weights, dtypes):
    vm = pl.BlockSpec(memory_space=pltpu.VMEM)
    count, tokens = len(rows), rows[0].shape[0]
    return pl.pallas_call(
        lambda *refs: product_kernel(count, *refs),
        in_specs=[vm] * (count + len(weights)),
        out_specs=[vm] * count,
        out_shape=[jax.ShapeDtypeStruct((tokens, 1024), dtype) for dtype in dtypes],
        compiler_params=pltpu.CompilerParams(vmem_limit_bytes=24 * 1024 * 1024),
        cost_estimate=pl.CostEstimate(
            flops=count * tokens * 2048 * 2048, bytes_accessed=4 << 20, transcendentals=0
        ),
        name="products",
    )(*rows, *weights)


def kv_kernel(j_ref, own_ref, r1_ref, r3_ref, r2_ref, bias_ref, cos_ref, sin_ref, *outs):
    j = j_ref[0]

    def part(col):
        cols = pl.ds(pl.multiple_of(col, 128), 128)
        back = r1_ref[:, cols].astype(F32) + r3_ref[:, cols].astype(F32) + r2_ref[:, cols].astype(F32)
        return own_ref[:, cols] + back + bias_ref[:, cols]

    for k in range(4):
        head = j ^ k
        key = part(head * HD)
        turned = key * cos_ref[...] + pltpu.roll(key, HD // 2, 1) * sin_ref[...]
        outs[k][:, :HD] = turned.astype(BF)
        outs[k][:, HD:] = part(KVH * HD + head * HD).astype(BF)


def kv_call(j, own, r1, r3, r2, bias, cos, sin):
    vm = pl.BlockSpec(memory_space=pltpu.VMEM)
    return pl.pallas_call(
        kv_kernel,
        in_specs=[pl.BlockSpec(memory_space=pltpu.SMEM)] + [vm] * 7,
        out_specs=[vm] * 4,
        out_shape=[jax.ShapeDtypeStruct((own.shape[0], 2 * HD), BF)] * 4,
        compiler_params=pltpu.CompilerParams(vmem_limit_bytes=8 * 1024 * 1024),
        cost_estimate=pl.CostEstimate(flops=1 << 20, bytes_accessed=2 << 20, transcendentals=0),
        name="keys_values",
    )(j, own, r1, r3, r2, bias, cos, sin)


def visit(pair, q_ref, pieces, reach, top, acc, fresh=False):
    parts = [ref[pl.ds(row, 256), :] for ref, row in pieces]
    width = 256 * len(parts)
    keys = jnp.concatenate([p[:, :HD] for p in parts], axis=0)
    values = jnp.concatenate([p[:, HD:] for p in parts], axis=0)
    values = jnp.concatenate([values, jnp.ones((width, HD), BF)], axis=1)
    for b in range(2):
        block = pair * 2 + b
        for h in range(0, H // KVH, 4):
            q = jnp.concatenate([q_ref[block, :, (h + i) * HD : (h + i + 1) * HD] for i in range(4)], axis=0)
            s = lax.dot_general(q, keys, (((1,), (1,)), ((), ())), preferred_element_type=F32)
            if reach is not None:
                col = lax.broadcasted_iota(jnp.int32, (BLK, BLK), 1)
                valid = jnp.concatenate([col <= r for r in reach[b]], axis=1)
                s = jnp.where(jnp.concatenate([valid] * 4, axis=0), s, LOW)
            rows = slice(h * BLK, (h + 4) * BLK)
            peak = jnp.max(s, axis=-1, keepdims=True)
            if fresh:
                new = jnp.broadcast_to(peak, (4 * BLK, HD))
            else:
                old = top[block, rows]
                new = jnp.maximum(old, peak)
            top[block, rows] = new
            shift = new if reach is None else jnp.maximum(new, LOW / 2)
            p = jnp.exp2((s - jnp.concatenate([shift] * (width // HD), axis=1)) * SCALE)
            add = jnp.dot(p.astype(BF), values, preferred_element_type=F32)
            if fresh:
                acc[block, rows] = add
            else:
                factor = jnp.exp2((old - new) * SCALE)
                acc[block, rows] = acc[block, rows] * jnp.concatenate([factor, factor], axis=1) + add


def reaches(flag_ref, pair, blocks):
    row = lax.broadcasted_iota(jnp.int32, (BLK, BLK), 0)
    out = []
    for b in range(2):
        flags = [flag_ref[pair * 2 + b, u] for u in blocks]
        out.append([jnp.where(f == 2, row, jnp.where(f == 1, BLK, -1)) for f in flags])
    return out


def flag_sum(flag_ref, pair, blocks):
    return sum(flag_ref[pair * 2 + b, u] for b in range(2) for u in blocks)


def all_whole(flag_ref, pair, blocks):
    whole = True
    for b in range(2):
        for u in blocks:
            whole = (flag_ref[pair * 2 + b, u] == 1) & whole
    return whole


def attend_source(flag_ref, source, pair, q_ref, pieces, top, acc):
    blocks = [source * 4 + i for i in range(4)]
    whole = all_whole(flag_ref, pair, blocks)

    @pl.when(whole)
    def _():
        visit(pair, q_ref, pieces, None, top, acc)

    for i in range(2):
        half = blocks[2 * i : 2 * i + 2]

        @pl.when(jnp.logical_not(whole) & (flag_sum(flag_ref, pair, half) > 0))
        def _(i=i, half=half):
            visit(pair, q_ref, pieces[i : i + 1], reaches(flag_ref, pair, half), top, acc)


def attend_first_kernel(flag_ref, q_ref, kv_ref, top, acc):
    def step(pair, carry):
        other = flag_sum(flag_ref, pair, [(1 - pair) * 2, (1 - pair) * 2 + 1])
        both = other > 0

        @pl.when(both)
        def _():
            visit(pair, q_ref, [(kv_ref, 0), (kv_ref, 256)], reaches(flag_ref, pair, range(4)), top, acc, True)

        @pl.when(jnp.logical_not(both))
        def _():
            row = pl.multiple_of(pair * 256, 256)
            mine = [pair * 2, pair * 2 + 1]
            visit(pair, q_ref, [(kv_ref, row)], reaches(flag_ref, pair, mine), top, acc, True)

        return carry

    lax.fori_loop(0, 2, step, 0)


def attend_more_kernel(flag_ref, q_ref, up_ref, down_ref, top_in, acc_in, top, acc):
    def step(pair, carry):
        for source, ref in ((1, up_ref), (2, down_ref)):
            attend_source(flag_ref, source, pair, q_ref, [(ref, 0), (ref, 256)], top, acc)
        return carry

    lax.fori_loop(0, 2, step, 0)


def attend_last_kernel(pair, flag_ref, q_ref, far0_ref, far1_ref, top_in, acc_in, top, acc, *outs):
    attend_source(flag_ref, 3, pair, q_ref, [(far0_ref, 0), (far1_ref, 0)], top, acc)
    for b in range(2):
        for h in range(H // KVH):
            rows = slice(h * BLK, (h + 1) * BLK)
            mixed = acc[pair * 2 + b, rows]
            outs[b][:, h * HD : (h + 1) * HD] = (mixed[:, :HD] / mixed[:, HD:]).astype(BF)


STATE = [
    jax.ShapeDtypeStruct((4, GW, HD), F32),
    jax.ShapeDtypeStruct((4, GW, 2 * HD), F32),
]


def attend_call(kernel, flags, arrays, outs, aliases=None, share=1, name="attend"):
    vm = pl.BlockSpec(memory_space=pltpu.VMEM)
    return pl.pallas_call(
        kernel,
        in_specs=[pl.BlockSpec(memory_space=pltpu.SMEM)] + [vm] * len(arrays),
        out_specs=[vm] * len(outs),
        out_shape=outs,
        input_output_aliases=aliases or {},
        compiler_params=pltpu.CompilerParams(vmem_limit_bytes=24 * 1024 * 1024),
        cost_estimate=pl.CostEstimate(flops=share << 30, bytes_accessed=4 << 20, transcendentals=share << 20),
        name=name,
    )(flags, *arrays)


def place_kernel(j_ref, *refs):
    out_ref = refs[-1]
    for k in range(4):
        cols = pl.ds(pl.multiple_of((j_ref[0] ^ k) * GW, GW), GW)
        out_ref[:, cols] = refs[k][...]


def place_call(j, parts):
    vm = pl.BlockSpec(memory_space=pltpu.VMEM)
    return pl.pallas_call(
        place_kernel,
        in_specs=[pl.BlockSpec(memory_space=pltpu.SMEM)] + [vm] * 4,
        out_specs=vm,
        out_shape=jax.ShapeDtypeStruct((BLK, H * HD), BF),
        compiler_params=pltpu.CompilerParams(vmem_limit_bytes=8 * 1024 * 1024),
        name="place",
    )(j, *parts)


def rotary_tables(start, count):
    half_dim = HD // 2
    positions = start + jnp.arange(count, dtype=jnp.int32)
    inv_freq = jnp.exp(jnp.arange(half_dim, dtype=F32) * (-2.0 * math.log(1000000.0) / HD))
    angle = positions.astype(F32)[:, None] * inv_freq[None, :]
    cosine, sine = jnp.cos(angle), jnp.sin(angle)
    return jnp.concatenate([cosine, cosine], 1), jnp.concatenate([-sine, sine], 1)


def after(value, earlier):
    return lax.optimization_barrier((value, earlier))[0]


def on_device(hidden_in, queries, kv_weight, kv_bias, norm_gain, block_mask):
    f = lax.axis_index("fsdp")
    c = lax.axis_index("ctx")
    core, xi, yhi = f & 1, (f >> 1) & 3, f >> 3
    z, ylo = c & 7, c >> 3
    j = ylo * 2 + (z & 1)
    zq = z >> 1
    hidden = hidden_in.reshape(BLK, D)
    q = queries.reshape(BLK, H * HD)
    j1 = jnp.reshape(j, (1,))

    pos = jnp.stack([xi, yhi, core])
    gain = norm_gain.reshape(1, D)
    w_y = lax.ppermute(kv_weight, ("ctx", "fsdp"), DIAG_PAIRS)

    normed0, normed1, normed2, normed3 = norm_call(pos, hidden, gain)
    n2 = lax.ppermute(normed2, "fsdp", x_pairs(2))
    n1 = lax.ppermute(normed1, "fsdp", x_pairs(1))
    n3 = lax.ppermute(normed3, "fsdp", x_pairs(3))
    q_parts = [lax.dynamic_slice(q, (0, (j ^ k) * GW), (BLK, GW)) for k in range(4)]
    q_parts[2] = lax.ppermute(after(q_parts[2], normed0), "ctx", member_pairs(2))
    q_parts[3] = lax.ppermute(after(q_parts[3], q_parts[2]), "ctx", member_pairs(3))
    w_core = lax.ppermute(after(kv_weight, q_parts[3]), "fsdp", CORE_PAIRS)
    w_yc = lax.ppermute(after(w_y, q_parts[3]), "fsdp", CORE_PAIRS)
    q_parts[1] = lax.ppermute(after(q_parts[1], w_core), "ctx", member_pairs(1))
    q4 = jnp.stack(q_parts)

    weights = [kv_weight, w_core, w_y, w_yc]
    p1, p3, p2, own = product_call([n1, n3, n2, normed0], weights, [BF, BF, BF, F32])
    back = [lax.ppermute(p, "fsdp", x_pairs(k)) for p, k in ((p1, 3), (p3, 1), (p2, 2))]

    cos, sin = rotary_tables(c * BLK, BLK)
    kvs = kv_call(j1, own, back[0], back[1], back[2], kv_bias.reshape(1, -1), cos, sin)
    group = jnp.concatenate([kvs[0]] + [lax.ppermute(kvs[k], "ctx", member_pairs(k)) for k in (1, 2, 3)], axis=0)

    up = lax.ppermute(group, "ctx", z_pairs(2))
    down = lax.ppermute(group, "ctx", z_pairs(-2))
    far0 = lax.ppermute(up[:256], "ctx", z_pairs(2))
    far1 = lax.ppermute(down[256:], "ctx", z_pairs(-2))

    members = j ^ jnp.arange(4, dtype=jnp.int32)
    block_of = lambda at: (members >> 1) * 8 + 2 * at + (members & 1)
    q_ids = block_of(zq)
    u_ids = jnp.concatenate([q_ids, block_of((zq + 3) & 3), block_of((zq + 1) & 3), block_of((zq + 2) & 3)])
    table = block_mask.reshape(16, 16)
    seen = jnp.take(jnp.take(table, q_ids, axis=0), u_ids, axis=1) == 1
    order = q_ids[:, None] - u_ids[None, :]
    flags = jnp.where(order == 0, 2, jnp.where(order > 0, 1, 0)) * seen.astype(jnp.int32)

    flags = flags.astype(jnp.int32)

    top, acc = attend_call(attend_first_kernel, flags, [q4, group], STATE, share=1, name="attend_first")
    top, acc = attend_call(
        attend_more_kernel, flags, [q4, up, down, top, acc], STATE, aliases={4: 0, 5: 1}, share=3, name="attend_more"
    )

    def finish(pair, top, acc, share, name):
        return attend_call(
            lambda *refs: attend_last_kernel(pair, *refs),
            flags,
            [q4, far0, far1, top, acc],
            STATE + [jax.ShapeDtypeStruct((BLK, GW), BF)] * 2,
            aliases={4: 0, 5: 1},
            share=share,
            name=name,
        )

    top, acc, out2, out3 = finish(1, top, acc, 1, "attend_others")
    top, acc, out0, out1 = finish(0, top, acc, 16, "attend_own")
    parts = [out0] + [lax.ppermute(o, "ctx", member_pairs(k)) for k, o in ((1, out1), (2, out2), (3, out3))]
    return place_call(j1, parts).reshape(1, BLK, H * HD)


def solution(mesh):
    return jax.shard_map(
        on_device,
        mesh=mesh,
        in_specs=(
            P("fsdp", "ctx", None),
            P("fsdp", "ctx", None),
            P("fsdp", None),
            P(),
            P(),
            P("fsdp", None, None),
        ),
        out_specs=P("fsdp", "ctx", None),
        check_vma=False,
    )
```

```python
import math

import jax
import jax.numpy as jnp
from jax import lax
from jax.experimental import pallas as pl
from jax.experimental.pallas import tpu as pltpu
from jax.sharding import PartitionSpec as P

H = 32
KVH = 4
HD = 128
BLK = 128
D = 8192
GW = (H // KVH) * HD
LOW = -1e30
SCALE = math.log2(math.e) / math.sqrt(HD)
BF = jnp.bfloat16
F32 = jnp.float32


def x_pairs(k):
    return [(f, (f & 8) | ((((f >> 1) + k) & 3) << 1) | (f & 1)) for f in range(16)]


CORE_PAIRS = [(f, f ^ 1) for f in range(16)]
DIAG_PAIRS = [(i, i ^ (8 * 16) ^ 8) for i in range(256)]


def member_pairs(k):
    flip = ((k >> 1) << 3) | (k & 1)
    return [(c, c ^ flip) for c in range(16)]


def z_pairs(k):
    return [(c, (c & 8) | ((c + k) & 7)) for c in range(16)]


def part_column(pos_ref, k, i):
    a, b = i >> 1, i & 1
    src = (pos_ref[1] ^ a) * 4096 + ((pos_ref[0] + k) & 3) * 1024 + (pos_ref[2] ^ b) * 512
    return pl.multiple_of(src, 512)


def norm_kernel(pos_ref, x_hbm, gain_hbm, q_hbm, out0, out1, out2, out3, q0, q1, q2, q3, x_ref, gain_ref, sems):
    step = 32
    count = x_ref.shape[0] // step
    copies = [
        pltpu.make_async_copy(
            x_hbm.at[pl.ds(i * step, step)], x_ref.at[pl.ds(i * step, step)], sems.at[i]
        )
        for i in range(count)
    ]
    gain_copy = pltpu.make_async_copy(gain_hbm, gain_ref, sems.at[count])
    copies[0].start()
    gain_copy.start()
    for copy in copies[1:]:
        copy.start()
    q_copies = []
    for k, out in ((2, q2), (3, q3), (1, q1), (0, q0)):
        cols = pl.ds(pl.multiple_of((pos_ref[3] ^ k) * GW, GW), GW)
        q_copies.append(pltpu.make_async_copy(q_hbm.at[:, cols], out, sems.at[count + 1 + k]))
        q_copies[-1].start()
    for n in range(count):
        copies[n].wait()
        if n == 0:
            gain_copy.wait()
        rows = slice(n * step, (n + 1) * step)
        total = None
        for j in range(D // 128):
            part = x_ref[rows, j * 128 : (j + 1) * 128].astype(F32)
            part = part * part
            total = part if total is None else total + part
        inv = lax.rsqrt(jnp.sum(total, axis=-1, keepdims=True) / D + 1e-06)
        for k, out in ((2, out2), (1, out1), (3, out3), (0, out0)):
            for i in range(4):
                cols = pl.ds(part_column(pos_ref, k, i), 512)
                wide = x_ref[rows, cols].astype(F32)
                out[rows, i * 512 : (i + 1) * 512] = (wide * inv * gain_ref[:, cols]).astype(BF)
    for copy in q_copies:
        copy.wait()


def norm_call(pos, hidden, gain, q):
    rows = hidden.shape[0]
    vm = pl.BlockSpec(memory_space=pltpu.VMEM)
    hbm = pl.BlockSpec(memory_space=pl.ANY)
    return pl.pallas_call(
        norm_kernel,
        in_specs=[pl.BlockSpec(memory_space=pltpu.SMEM), hbm, hbm, hbm],
        out_specs=[vm] * 8,
        out_shape=[jax.ShapeDtypeStruct((rows, D // 4), BF)] * 4 + [jax.ShapeDtypeStruct((rows, GW), BF)] * 4,
        scratch_shapes=[
            pltpu.VMEM((rows, D), BF),
            pltpu.VMEM((1, D), F32),
            pltpu.SemaphoreType.DMA((rows // 32 + 5,)),
        ],
        compiler_params=pltpu.CompilerParams(vmem_limit_bytes=50 * 1024 * 1024),
        cost_estimate=pl.CostEstimate(flops=4 << 20, bytes_accessed=4 << 20, transcendentals=0),
        name="norm",
    )(pos, hidden, gain, q)


def product_kernel(count, *refs):
    rows, weights, outs = refs[:count], refs[count:-count], refs[-count:]
    tokens = rows[0].shape[0]
    left = jnp.concatenate([r[...] for r in rows], axis=0)
    right = jnp.concatenate([w[...] for w in weights], axis=0)
    total = jnp.dot(left, right, preferred_element_type=F32)
    for i in range(count):
        outs[i][...] = total[i * tokens : (i + 1) * tokens].astype(outs[i].dtype)


def product_call(rows, weights, dtype, name):
    vm = pl.BlockSpec(memory_space=pltpu.VMEM)
    count, tokens = len(rows), rows[0].shape[0]
    return pl.pallas_call(
        lambda *refs: product_kernel(count, *refs),
        in_specs=[vm] * (count + len(weights)),
        out_specs=[vm] * count,
        out_shape=[jax.ShapeDtypeStruct((tokens, 1024), dtype)] * count,
        compiler_params=pltpu.CompilerParams(vmem_limit_bytes=24 * 1024 * 1024),
        cost_estimate=pl.CostEstimate(
            flops=count * tokens * 2048 * 2048, bytes_accessed=4 << 20, transcendentals=0
        ),
        name=name,
    )(*rows, *weights)


def kv_kernel(j_ref, own_ref, r1_ref, r3_ref, r2_ref, bias_ref, cos_ref, sin_ref, *outs):
    j = j_ref[0]

    def part(col):
        cols = pl.ds(pl.multiple_of(col, 128), 128)
        back = r1_ref[:, cols].astype(F32) + r3_ref[:, cols].astype(F32) + r2_ref[:, cols].astype(F32)
        return own_ref[:, cols] + back + bias_ref[:, cols]

    for k in range(4):
        head = j ^ k
        key = part(head * HD)
        turned = key * cos_ref[...] + pltpu.roll(key, HD // 2, 1) * sin_ref[...]
        outs[k][:, :HD] = turned.astype(BF)
        outs[k][:, HD:] = part(KVH * HD + head * HD).astype(BF)


def kv_call(j, own, r1, r3, r2, bias, cos, sin):
    vm = pl.BlockSpec(memory_space=pltpu.VMEM)
    return pl.pallas_call(
        kv_kernel,
        in_specs=[pl.BlockSpec(memory_space=pltpu.SMEM)] + [vm] * 7,
        out_specs=[vm] * 4,
        out_shape=[jax.ShapeDtypeStruct((own.shape[0], 2 * HD), BF)] * 4,
        compiler_params=pltpu.CompilerParams(vmem_limit_bytes=8 * 1024 * 1024),
        cost_estimate=pl.CostEstimate(flops=1 << 20, bytes_accessed=2 << 20, transcendentals=0),
        name="keys_values",
    )(j, own, r1, r3, r2, bias, cos, sin)


def visit(pair, q_ref, pieces, reach, top, acc, fresh=False):
    parts = [ref[pl.ds(row, 256), :] for ref, row in pieces]
    width = 256 * len(parts)
    keys = jnp.concatenate([p[:, :HD] for p in parts], axis=0)
    values = jnp.concatenate([p[:, HD:] for p in parts], axis=0)
    values = jnp.concatenate([values, jnp.ones((width, HD), BF)], axis=1)
    for b in range(2):
        block = pair * 2 + b
        for h in range(0, H // KVH, 4):
            q = jnp.concatenate([q_ref[block, :, (h + i) * HD : (h + i + 1) * HD] for i in range(4)], axis=0)
            s = lax.dot_general(q, keys, (((1,), (1,)), ((), ())), preferred_element_type=F32)
            if reach is not None:
                col = lax.broadcasted_iota(jnp.int32, (BLK, BLK), 1)
                valid = jnp.concatenate([col <= r for r in reach[b]], axis=1)
                s = jnp.where(jnp.concatenate([valid] * 4, axis=0), s, LOW)
            rows = slice(h * BLK, (h + 4) * BLK)
            peak = jnp.max(s, axis=-1, keepdims=True)
            if fresh:
                new = jnp.broadcast_to(peak, (4 * BLK, HD))
            else:
                old = top[block, rows]
                new = jnp.maximum(old, peak)
            top[block, rows] = new
            shift = new if reach is None else jnp.maximum(new, LOW / 2)
            p = jnp.exp2((s - jnp.concatenate([shift] * (width // HD), axis=1)) * SCALE)
            add = jnp.dot(p.astype(BF), values, preferred_element_type=F32)
            if fresh:
                acc[block, rows] = add
            else:
                factor = jnp.exp2((old - new) * SCALE)
                acc[block, rows] = acc[block, rows] * jnp.concatenate([factor, factor], axis=1) + add


def reaches(flag_ref, pair, blocks):
    row = lax.broadcasted_iota(jnp.int32, (BLK, BLK), 0)
    out = []
    for b in range(2):
        flags = [flag_ref[pair * 2 + b, u] for u in blocks]
        out.append([jnp.where(f == 2, row, jnp.where(f == 1, BLK, -1)) for f in flags])
    return out


def flag_sum(flag_ref, pair, blocks):
    return sum(flag_ref[pair * 2 + b, u] for b in range(2) for u in blocks)


def all_whole(flag_ref, pair, blocks):
    whole = True
    for b in range(2):
        for u in blocks:
            whole = (flag_ref[pair * 2 + b, u] == 1) & whole
    return whole


def attend_source(flag_ref, source, pair, q_ref, pieces, top, acc):
    blocks = [source * 4 + i for i in range(4)]
    whole = all_whole(flag_ref, pair, blocks)

    @pl.when(whole)
    def _():
        visit(pair, q_ref, pieces, None, top, acc)

    for i in range(2):
        half = blocks[2 * i : 2 * i + 2]

        @pl.when(jnp.logical_not(whole) & (flag_sum(flag_ref, pair, half) > 0))
        def _(i=i, half=half):
            visit(pair, q_ref, pieces[i : i + 1], reaches(flag_ref, pair, half), top, acc)


def attend_first_kernel(flag_ref, q_ref, kv_ref, top, acc):
    def step(pair, carry):
        other = flag_sum(flag_ref, pair, [(1 - pair) * 2, (1 - pair) * 2 + 1])
        both = other > 0

        @pl.when(both)
        def _():
            visit(pair, q_ref, [(kv_ref, 0), (kv_ref, 256)], reaches(flag_ref, pair, range(4)), top, acc, True)

        @pl.when(jnp.logical_not(both))
        def _():
            row = pl.multiple_of(pair * 256, 256)
            mine = [pair * 2, pair * 2 + 1]
            visit(pair, q_ref, [(kv_ref, row)], reaches(flag_ref, pair, mine), top, acc, True)

        return carry

    lax.fori_loop(0, 2, step, 0)


def attend_more_kernel(flag_ref, q_ref, up_ref, down_ref, top_in, acc_in, top, acc):
    def step(pair, carry):
        for source, ref in ((1, up_ref), (2, down_ref)):
            attend_source(flag_ref, source, pair, q_ref, [(ref, 0), (ref, 256)], top, acc)
        return carry

    lax.fori_loop(0, 2, step, 0)


def attend_last_kernel(pair, flag_ref, q_ref, far0_ref, far1_ref, top_in, acc_in, top, acc, *outs):
    attend_source(flag_ref, 3, pair, q_ref, [(far0_ref, 0), (far1_ref, 0)], top, acc)
    for b in range(2):
        for h in range(H // KVH):
            rows = slice(h * BLK, (h + 1) * BLK)
            mixed = acc[pair * 2 + b, rows]
            outs[b][:, h * HD : (h + 1) * HD] = (mixed[:, :HD] / mixed[:, HD:]).astype(BF)


STATE = [
    jax.ShapeDtypeStruct((4, GW, HD), F32),
    jax.ShapeDtypeStruct((4, GW, 2 * HD), F32),
]


def attend_call(kernel, flags, arrays, outs, aliases=None, share=1, name="attend"):
    vm = pl.BlockSpec(memory_space=pltpu.VMEM)
    return pl.pallas_call(
        kernel,
        in_specs=[pl.BlockSpec(memory_space=pltpu.SMEM)] + [vm] * len(arrays),
        out_specs=[vm] * len(outs),
        out_shape=outs,
        input_output_aliases=aliases or {},
        compiler_params=pltpu.CompilerParams(vmem_limit_bytes=24 * 1024 * 1024),
        cost_estimate=pl.CostEstimate(flops=share << 30, bytes_accessed=4 << 20, transcendentals=share << 20),
        name=name,
    )(flags, *arrays)


def place_kernel(members, j_ref, *refs):
    parts, out_ref, sems = refs[: len(members)], refs[-2], refs[-1]
    copies = []
    for i, k in enumerate(members):
        cols = pl.ds(pl.multiple_of((j_ref[0] ^ k) * GW, GW), GW)
        copies.append(pltpu.make_async_copy(parts[i], out_ref.at[:, cols], sems.at[i]))
        copies[-1].start()
    for copy in copies:
        copy.wait()


def place_call(j, parts, members, out=None):
    vm = pl.BlockSpec(memory_space=pltpu.VMEM)
    hbm = pl.BlockSpec(memory_space=pl.ANY)
    return pl.pallas_call(
        lambda *refs: place_kernel(members, *refs),
        in_specs=[pl.BlockSpec(memory_space=pltpu.SMEM)] + [vm] * len(parts) + ([] if out is None else [hbm]),
        out_specs=hbm,
        out_shape=jax.ShapeDtypeStruct((BLK, H * HD), BF),
        scratch_shapes=[pltpu.SemaphoreType.DMA((len(members),))],
        input_output_aliases={} if out is None else {1 + len(parts): 0},
        compiler_params=pltpu.CompilerParams(vmem_limit_bytes=8 * 1024 * 1024),
        name="place",
    )(j, *parts, *([] if out is None else [out]))


def rotary_tables(start, count):
    half_dim = HD // 2
    positions = start + jnp.arange(count, dtype=jnp.int32)
    inv_freq = jnp.exp(jnp.arange(half_dim, dtype=F32) * (-2.0 * math.log(1000000.0) / HD))
    angle = positions.astype(F32)[:, None] * inv_freq[None, :]
    cosine, sine = jnp.cos(angle), jnp.sin(angle)
    return jnp.concatenate([cosine, cosine], 1), jnp.concatenate([-sine, sine], 1)


def after(value, earlier):
    return lax.optimization_barrier((value, earlier))[0]


def on_device(hidden_in, queries, kv_weight, kv_bias, norm_gain, block_mask):
    f = lax.axis_index("fsdp")
    c = lax.axis_index("ctx")
    core, xi, yhi = f & 1, (f >> 1) & 3, f >> 3
    z, ylo = c & 7, c >> 3
    j = ylo * 2 + (z & 1)
    zq = z >> 1
    hidden = hidden_in.reshape(BLK, D)
    q = queries.reshape(BLK, H * HD)
    j1 = jnp.reshape(j, (1,))

    pos = jnp.stack([xi, yhi, core, j])
    gain = norm_gain.reshape(1, D)
    w_y = lax.ppermute(kv_weight, ("ctx", "fsdp"), DIAG_PAIRS)

    normed0, normed1, normed2, normed3, *q_parts = norm_call(pos, hidden, gain, q)
    n2 = lax.ppermute(normed2, "fsdp", x_pairs(2))
    n1 = lax.ppermute(normed1, "fsdp", x_pairs(1))
    n3 = lax.ppermute(normed3, "fsdp", x_pairs(3))
    q_parts[2] = lax.ppermute(q_parts[2], "ctx", member_pairs(2))
    q_parts[3] = lax.ppermute(after(q_parts[3], q_parts[2]), "ctx", member_pairs(3))
    w_core = lax.ppermute(after(kv_weight, q_parts[3]), "fsdp", CORE_PAIRS)
    w_yc = lax.ppermute(after(w_y, q_parts[3]), "fsdp", CORE_PAIRS)
    q_parts[1] = lax.ppermute(after(q_parts[1], w_core), "ctx", member_pairs(1))
    q4 = jnp.stack(q_parts)

    weights = [kv_weight, w_core, w_y, w_yc]
    p1, p3 = product_call([n1, n3], weights, BF, "products")
    (p2,) = product_call([n2], weights, BF, "far_product")
    back = [lax.ppermute(p, "fsdp", x_pairs(k)) for p, k in ((p1, 3), (p3, 1), (p2, 2))]
    (own,) = product_call([normed0], weights, F32, "own_product")

    cos, sin = rotary_tables(c * BLK, BLK)
    kvs = kv_call(j1, own, back[0], back[1], back[2], kv_bias.reshape(1, -1), cos, sin)
    group = jnp.concatenate([kvs[0]] + [lax.ppermute(kvs[k], "ctx", member_pairs(k)) for k in (1, 2, 3)], axis=0)

    up = lax.ppermute(group, "ctx", z_pairs(2))
    down = lax.ppermute(group, "ctx", z_pairs(-2))
    far0 = lax.ppermute(up[:256], "ctx", z_pairs(2))
    far1 = lax.ppermute(down[256:], "ctx", z_pairs(-2))

    members = j ^ jnp.arange(4, dtype=jnp.int32)
    block_of = lambda at: (members >> 1) * 8 + 2 * at + (members & 1)
    q_ids = block_of(zq)
    u_ids = jnp.concatenate([q_ids, block_of((zq + 3) & 3), block_of((zq + 1) & 3), block_of((zq + 2) & 3)])
    table = block_mask.reshape(16, 16)
    seen = jnp.take(jnp.take(table, q_ids, axis=0), u_ids, axis=1) == 1
    order = q_ids[:, None] - u_ids[None, :]
    flags = jnp.where(order == 0, 2, jnp.where(order > 0, 1, 0)) * seen.astype(jnp.int32)

    flags = flags.astype(jnp.int32)

    top, acc = attend_call(attend_first_kernel, flags, [q4, group], STATE, share=1, name="attend_first")
    top, acc = attend_call(
        attend_more_kernel, flags, [q4, up, down, top, acc], STATE, aliases={4: 0, 5: 1}, share=3, name="attend_more"
    )

    def finish(pair, top, acc, name):
        return attend_call(
            lambda *refs: attend_last_kernel(pair, *refs),
            flags,
            [q4, far0, far1, top, acc],
            STATE + [jax.ShapeDtypeStruct((BLK, GW), BF)] * 2,
            aliases={4: 0, 5: 1},
            name=name,
        )

    top, acc, out2, out3 = finish(1, top, acc, "attend_others")
    top, acc, out0, out1 = finish(0, top, acc, "attend_own")
    got = [lax.ppermute(o, "ctx", member_pairs(k)) for k, o in ((3, out3), (2, out2), (1, out1))]
    placed = place_call(j1, [out0, got[2]], (0, 1))
    placed = place_call(j1, [got[1]], (2,), placed)
    return place_call(j1, [got[0]], (3,), placed).reshape(1, BLK, H * HD)


def solution(mesh):
    return jax.shard_map(
        on_device,
        mesh=mesh,
        in_specs=(
            P("fsdp", "ctx", None),
            P("fsdp", "ctx", None),
            P("fsdp", None),
            P(),
            P(),
            P("fsdp", None, None),
        ),
        out_specs=P("fsdp", "ctx", None),
        check_vma=False,
    )
```

```python
import math

import jax
import jax.numpy as jnp
from jax import lax
from jax.experimental import pallas as pl
from jax.experimental.pallas import tpu as pltpu
from jax.sharding import PartitionSpec as P

H = 32
KVH = 4
HD = 128
BLK = 128
D = 8192
GW = (H // KVH) * HD
LOW = -1e30
SCALE = math.log2(math.e) / math.sqrt(HD)
BF = jnp.bfloat16
F32 = jnp.float32


def x_pairs(k):
    return [(f, (f & 8) | ((((f >> 1) + k) & 3) << 1) | (f & 1)) for f in range(16)]


CORE_PAIRS = [(f, f ^ 1) for f in range(16)]
DIAG_PAIRS = [(i, i ^ (8 * 16) ^ 8) for i in range(256)]


def member_pairs(k):
    flip = ((k >> 1) << 3) | (k & 1)
    return [(c, c ^ flip) for c in range(16)]


def z_pairs(k):
    return [(c, (c & 8) | ((c + k) & 7)) for c in range(16)]


def part_column(pos_ref, k, i):
    a, b = i >> 1, i & 1
    src = (pos_ref[1] ^ a) * 4096 + ((pos_ref[0] + k) & 3) * 1024 + (pos_ref[2] ^ b) * 512
    return pl.multiple_of(src, 512)


def norm_kernel(pos_ref, x_hbm, gain_hbm, q_hbm, out0, out1, out2, out3, q0, q1, q2, q3, x_ref, gain_ref, sems):
    step = 32
    count = x_ref.shape[0] // step
    copies = [
        pltpu.make_async_copy(
            x_hbm.at[pl.ds(i * step, step)], x_ref.at[pl.ds(i * step, step)], sems.at[i]
        )
        for i in range(count)
    ]
    gain_copy = pltpu.make_async_copy(gain_hbm, gain_ref, sems.at[count])
    copies[0].start()
    gain_copy.start()
    for copy in copies[1:]:
        copy.start()
    q_copies = []
    for k, out in ((2, q2), (3, q3), (1, q1), (0, q0)):
        cols = pl.ds(pl.multiple_of((pos_ref[3] ^ k) * GW, GW), GW)
        q_copies.append(pltpu.make_async_copy(q_hbm.at[:, cols], out, sems.at[count + 1 + k]))
        q_copies[-1].start()
    for n in range(count):
        copies[n].wait()
        if n == 0:
            gain_copy.wait()
        rows = slice(n * step, (n + 1) * step)
        total = None
        for j in range(D // 128):
            part = x_ref[rows, j * 128 : (j + 1) * 128].astype(F32)
            part = part * part
            total = part if total is None else total + part
        inv = lax.rsqrt(jnp.sum(total, axis=-1, keepdims=True) / D + 1e-06)
        for k, out in ((2, out2), (1, out1), (3, out3), (0, out0)):
            for i in range(4):
                cols = pl.ds(part_column(pos_ref, k, i), 512)
                wide = x_ref[rows, cols].astype(F32)
                out[rows, i * 512 : (i + 1) * 512] = (wide * inv * gain_ref[:, cols]).astype(BF)
    for copy in q_copies:
        copy.wait()


def norm_call(pos, hidden, gain, q):
    rows = hidden.shape[0]
    vm = pl.BlockSpec(memory_space=pltpu.VMEM)
    hbm = pl.BlockSpec(memory_space=pl.ANY)
    return pl.pallas_call(
        norm_kernel,
        in_specs=[pl.BlockSpec(memory_space=pltpu.SMEM), hbm, hbm, hbm],
        out_specs=[vm] * 8,
        out_shape=[jax.ShapeDtypeStruct((rows, D // 4), BF)] * 4 + [jax.ShapeDtypeStruct((rows, GW), BF)] * 4,
        scratch_shapes=[
            pltpu.VMEM((rows, D), BF),
            pltpu.VMEM((1, D), F32),
            pltpu.SemaphoreType.DMA((rows // 32 + 5,)),
        ],
        compiler_params=pltpu.CompilerParams(vmem_limit_bytes=50 * 1024 * 1024),
        cost_estimate=pl.CostEstimate(flops=4 << 20, bytes_accessed=4 << 20, transcendentals=0),
        name="norm",
    )(pos, hidden, gain, q)


def product_kernel(count, *refs):
    rows, weights, outs = refs[:count], refs[count:-count], refs[-count:]
    tokens = rows[0].shape[0]
    left = jnp.concatenate([r[...] for r in rows], axis=0)
    right = jnp.concatenate([w[...] for w in weights], axis=0)
    total = jnp.dot(left, right, preferred_element_type=F32)
    for i in range(count):
        outs[i][...] = total[i * tokens : (i + 1) * tokens].astype(outs[i].dtype)


def product_call(rows, weights, dtype, name):
    vm = pl.BlockSpec(memory_space=pltpu.VMEM)
    count, tokens = len(rows), rows[0].shape[0]
    return pl.pallas_call(
        lambda *refs: product_kernel(count, *refs),
        in_specs=[vm] * (count + len(weights)),
        out_specs=[vm] * count,
        out_shape=[jax.ShapeDtypeStruct((tokens, 1024), dtype)] * count,
        compiler_params=pltpu.CompilerParams(vmem_limit_bytes=24 * 1024 * 1024),
        cost_estimate=pl.CostEstimate(
            flops=count * tokens * 2048 * 2048, bytes_accessed=4 << 20, transcendentals=0
        ),
        name=name,
    )(*rows, *weights)


def kv_kernel(j_ref, own_ref, r1_ref, r3_ref, r2_ref, bias_ref, cos_ref, sin_ref, *outs):
    j = j_ref[0]

    def part(col):
        cols = pl.ds(pl.multiple_of(col, 128), 128)
        back = r1_ref[:, cols].astype(F32) + r3_ref[:, cols].astype(F32) + r2_ref[:, cols].astype(F32)
        return own_ref[:, cols] + back + bias_ref[:, cols]

    for k in range(4):
        head = j ^ k
        key = part(head * HD)
        turned = key * cos_ref[...] + pltpu.roll(key, HD // 2, 1) * sin_ref[...]
        outs[k][:, :HD] = turned.astype(BF)
        outs[k][:, HD:] = part(KVH * HD + head * HD).astype(BF)


def kv_call(j, own, r1, r3, r2, bias, cos, sin):
    vm = pl.BlockSpec(memory_space=pltpu.VMEM)
    return pl.pallas_call(
        kv_kernel,
        in_specs=[pl.BlockSpec(memory_space=pltpu.SMEM)] + [vm] * 7,
        out_specs=[vm] * 4,
        out_shape=[jax.ShapeDtypeStruct((own.shape[0], 2 * HD), BF)] * 4,
        compiler_params=pltpu.CompilerParams(vmem_limit_bytes=8 * 1024 * 1024),
        cost_estimate=pl.CostEstimate(flops=1 << 20, bytes_accessed=2 << 20, transcendentals=0),
        name="keys_values",
    )(j, own, r1, r3, r2, bias, cos, sin)


def visit(pair, q_ref, pieces, reach, top, acc, fresh=False):
    parts = [ref[pl.ds(row, 256), :] for ref, row in pieces]
    width = 256 * len(parts)
    keys = jnp.concatenate([p[:, :HD] for p in parts], axis=0)
    values = jnp.concatenate([p[:, HD:] for p in parts], axis=0)
    values = jnp.concatenate([values, jnp.ones((width, HD), BF)], axis=1)
    for b in range(2):
        block = pair * 2 + b
        for h in range(0, H // KVH, 4):
            q = jnp.concatenate([q_ref[block, :, (h + i) * HD : (h + i + 1) * HD] for i in range(4)], axis=0)
            s = lax.dot_general(q, keys, (((1,), (1,)), ((), ())), preferred_element_type=F32)
            if reach is not None:
                col = lax.broadcasted_iota(jnp.int32, (BLK, BLK), 1)
                valid = jnp.concatenate([col <= r for r in reach[b]], axis=1)
                s = jnp.where(jnp.concatenate([valid] * 4, axis=0), s, LOW)
            rows = slice(h * BLK, (h + 4) * BLK)
            peak = jnp.max(s, axis=-1, keepdims=True)
            if fresh:
                new = jnp.broadcast_to(peak, (4 * BLK, HD))
            else:
                old = top[block, rows]
                new = jnp.maximum(old, peak)
            top[block, rows] = new
            shift = new if reach is None else jnp.maximum(new, LOW / 2)
            p = jnp.exp2((s - jnp.concatenate([shift] * (width // HD), axis=1)) * SCALE)
            add = jnp.dot(p.astype(BF), values, preferred_element_type=F32)
            if fresh:
                acc[block, rows] = add
            else:
                factor = jnp.exp2((old - new) * SCALE)
                acc[block, rows] = acc[block, rows] * jnp.concatenate([factor, factor], axis=1) + add


def reaches(flag_ref, pair, blocks):
    row = lax.broadcasted_iota(jnp.int32, (BLK, BLK), 0)
    out = []
    for b in range(2):
        flags = [flag_ref[pair * 2 + b, u] for u in blocks]
        out.append([jnp.where(f == 2, row, jnp.where(f == 1, BLK, -1)) for f in flags])
    return out


def flag_sum(flag_ref, pair, blocks):
    return sum(flag_ref[pair * 2 + b, u] for b in range(2) for u in blocks)


def all_whole(flag_ref, pair, blocks):
    whole = True
    for b in range(2):
        for u in blocks:
            whole = (flag_ref[pair * 2 + b, u] == 1) & whole
    return whole


def attend_source(flag_ref, source, pair, q_ref, pieces, top, acc):
    blocks = [source * 4 + i for i in range(4)]
    whole = all_whole(flag_ref, pair, blocks)

    @pl.when(whole)
    def _():
        visit(pair, q_ref, pieces, None, top, acc)

    for i in range(2):
        half = blocks[2 * i : 2 * i + 2]

        @pl.when(jnp.logical_not(whole) & (flag_sum(flag_ref, pair, half) > 0))
        def _(i=i, half=half):
            visit(pair, q_ref, pieces[i : i + 1], reaches(flag_ref, pair, half), top, acc)


def attend_first_kernel(flag_ref, q_ref, kv_ref, top, acc):
    def step(pair, carry):
        other = flag_sum(flag_ref, pair, [(1 - pair) * 2, (1 - pair) * 2 + 1])
        both = other > 0

        @pl.when(both)
        def _():
            visit(pair, q_ref, [(kv_ref, 0), (kv_ref, 256)], reaches(flag_ref, pair, range(4)), top, acc, True)

        @pl.when(jnp.logical_not(both))
        def _():
            row = pl.multiple_of(pair * 256, 256)
            mine = [pair * 2, pair * 2 + 1]
            visit(pair, q_ref, [(kv_ref, row)], reaches(flag_ref, pair, mine), top, acc, True)

        return carry

    lax.fori_loop(0, 2, step, 0)


def attend_more_kernel(flag_ref, q_ref, up_ref, down_ref, top_in, acc_in, top, acc):
    def step(pair, carry):
        for source, ref in ((1, up_ref), (2, down_ref)):
            attend_source(flag_ref, source, pair, q_ref, [(ref, 0), (ref, 256)], top, acc)
        return carry

    lax.fori_loop(0, 2, step, 0)


def attend_last_kernel(pair, flag_ref, q_ref, far0_ref, far1_ref, top_in, acc_in, top, acc, *outs):
    attend_source(flag_ref, 3, pair, q_ref, [(far0_ref, 0), (far1_ref, 0)], top, acc)
    for b in range(2):
        for h in range(H // KVH):
            rows = slice(h * BLK, (h + 1) * BLK)
            mixed = acc[pair * 2 + b, rows]
            outs[b][:, h * HD : (h + 1) * HD] = (mixed[:, :HD] / mixed[:, HD:]).astype(BF)


STATE = [
    jax.ShapeDtypeStruct((4, GW, HD), F32),
    jax.ShapeDtypeStruct((4, GW, 2 * HD), F32),
]


def attend_call(kernel, flags, arrays, outs, aliases=None, share=1, name="attend"):
    vm = pl.BlockSpec(memory_space=pltpu.VMEM)
    return pl.pallas_call(
        kernel,
        in_specs=[pl.BlockSpec(memory_space=pltpu.SMEM)] + [vm] * len(arrays),
        out_specs=[vm] * len(outs),
        out_shape=outs,
        input_output_aliases=aliases or {},
        compiler_params=pltpu.CompilerParams(vmem_limit_bytes=24 * 1024 * 1024),
        cost_estimate=pl.CostEstimate(flops=share << 30, bytes_accessed=4 << 20, transcendentals=share << 20),
        name=name,
    )(flags, *arrays)


def place_kernel(members, j_ref, *refs):
    parts, out_ref, sems = refs[: len(members)], refs[-2], refs[-1]
    copies = []
    for i, k in enumerate(members):
        cols = pl.ds(pl.multiple_of((j_ref[0] ^ k) * GW, GW), GW)
        copies.append(pltpu.make_async_copy(parts[i], out_ref.at[:, cols], sems.at[i]))
        copies[-1].start()
    for copy in copies:
        copy.wait()


def place_call(j, parts, members, out=None):
    vm = pl.BlockSpec(memory_space=pltpu.VMEM)
    hbm = pl.BlockSpec(memory_space=pl.ANY)
    return pl.pallas_call(
        lambda *refs: place_kernel(members, *refs),
        in_specs=[pl.BlockSpec(memory_space=pltpu.SMEM)] + [vm] * len(parts) + ([] if out is None else [hbm]),
        out_specs=hbm,
        out_shape=jax.ShapeDtypeStruct((BLK, H * HD), BF),
        scratch_shapes=[pltpu.SemaphoreType.DMA((len(members),))],
        input_output_aliases={} if out is None else {1 + len(parts): 0},
        compiler_params=pltpu.CompilerParams(vmem_limit_bytes=8 * 1024 * 1024),
        name="place",
    )(j, *parts, *([] if out is None else [out]))


def rotary_tables(start, count):
    half_dim = HD // 2
    positions = start + jnp.arange(count, dtype=jnp.int32)
    inv_freq = jnp.exp(jnp.arange(half_dim, dtype=F32) * (-2.0 * math.log(1000000.0) / HD))
    angle = positions.astype(F32)[:, None] * inv_freq[None, :]
    cosine, sine = jnp.cos(angle), jnp.sin(angle)
    return jnp.concatenate([cosine, cosine], 1), jnp.concatenate([-sine, sine], 1)


def after(value, earlier):
    return lax.optimization_barrier((value, earlier))[0]


def on_device(hidden_in, queries, kv_weight, kv_bias, norm_gain, block_mask):
    f = lax.axis_index("fsdp")
    c = lax.axis_index("ctx")
    core, xi, yhi = f & 1, (f >> 1) & 3, f >> 3
    z, ylo = c & 7, c >> 3
    j = ylo * 2 + (z & 1)
    zq = z >> 1
    hidden = hidden_in.reshape(BLK, D)
    q = queries.reshape(BLK, H * HD)
    j1 = jnp.reshape(j, (1,))

    pos = jnp.stack([xi, yhi, core, j])
    gain = norm_gain.reshape(1, D)
    w_y = lax.ppermute(kv_weight, ("ctx", "fsdp"), DIAG_PAIRS)

    normed0, normed1, normed2, normed3, *q_parts = norm_call(pos, hidden, gain, q)
    n1 = lax.ppermute(normed1, "fsdp", x_pairs(1))
    n3 = lax.ppermute(normed3, "fsdp", x_pairs(3))
    w_core = lax.ppermute(kv_weight, "fsdp", CORE_PAIRS)
    n2 = lax.ppermute(normed2, "fsdp", x_pairs(2))

    q_parts[2] = lax.ppermute(after(q_parts[2], w_core), "ctx", member_pairs(2))
    q_parts[3] = lax.ppermute(after(q_parts[3], q_parts[2]), "ctx", member_pairs(3))
    w_yc = lax.ppermute(after(w_y, q_parts[3]), "fsdp", CORE_PAIRS)
    q_parts[1] = lax.ppermute(after(q_parts[1], q_parts[3]), "ctx", member_pairs(1))
    q4 = jnp.stack(q_parts)

    weights = [kv_weight, w_core, w_y, w_yc]
    p1, p3 = product_call([n1, n3], weights, BF, "products")
    (p2,) = product_call([n2], weights, BF, "far_product")
    back = [lax.ppermute(p, "fsdp", x_pairs(k)) for p, k in ((p1, 3), (p3, 1), (p2, 2))]
    (own,) = product_call([normed0], weights, F32, "own_product")

    cos, sin = rotary_tables(c * BLK, BLK)
    kvs = kv_call(j1, own, back[0], back[1], back[2], kv_bias.reshape(1, -1), cos, sin)
    group = jnp.concatenate([kvs[0]] + [lax.ppermute(kvs[k], "ctx", member_pairs(k)) for k in (1, 2, 3)], axis=0)

    up = lax.ppermute(group, "ctx", z_pairs(2))
    down = lax.ppermute(group, "ctx", z_pairs(-2))
    far0 = lax.ppermute(up[:256], "ctx", z_pairs(2))
    far1 = lax.ppermute(down[256:], "ctx", z_pairs(-2))

    members = j ^ jnp.arange(4, dtype=jnp.int32)
    block_of = lambda at: (members >> 1) * 8 + 2 * at + (members & 1)
    q_ids = block_of(zq)
    u_ids = jnp.concatenate([q_ids, block_of((zq + 3) & 3), block_of((zq + 1) & 3), block_of((zq + 2) & 3)])
    table = block_mask.reshape(16, 16)
    seen = jnp.take(jnp.take(table, q_ids, axis=0), u_ids, axis=1) == 1
    order = q_ids[:, None] - u_ids[None, :]
    flags = jnp.where(order == 0, 2, jnp.where(order > 0, 1, 0)) * seen.astype(jnp.int32)

    flags = flags.astype(jnp.int32)

    top, acc = attend_call(attend_first_kernel, flags, [q4, group], STATE, share=1, name="attend_first")
    top, acc = attend_call(
        attend_more_kernel, flags, [q4, up, down, top, acc], STATE, aliases={4: 0, 5: 1}, share=3, name="attend_more"
    )

    def finish(pair, top, acc, name):
        return attend_call(
            lambda *refs: attend_last_kernel(pair, *refs),
            flags,
            [q4, far0, far1, top, acc],
            STATE + [jax.ShapeDtypeStruct((BLK, GW), BF)] * 2,
            aliases={4: 0, 5: 1},
            name=name,
        )

    top, acc, out2, out3 = finish(1, top, acc, "attend_others")
    top, acc, out0, out1 = finish(0, top, acc, "attend_own")
    got = [lax.ppermute(o, "ctx", member_pairs(k)) for k, o in ((3, out3), (2, out2), (1, out1))]
    placed = place_call(j1, [out0, got[2]], (0, 1))
    placed = place_call(j1, [got[1]], (2,), placed)
    return place_call(j1, [got[0]], (3,), placed).reshape(1, BLK, H * HD)


def solution(mesh):
    return jax.shard_map(
        on_device,
        mesh=mesh,
        in_specs=(
            P("fsdp", "ctx", None),
            P("fsdp", "ctx", None),
            P("fsdp", None),
            P(),
            P(),
            P("fsdp", None, None),
        ),
        out_specs=P("fsdp", "ctx", None),
        check_vma=False,
    )
```
